128 devices in a mesh: branch: 16 (over z_hi, x, core), head: 8 (over z_lo, y).
Axes of the slice: x: 4, y: 4, z: 4 (z_hi: 2, z_lo: 2; z = z_hi * 2 + z_lo), core: 2. Of those that a mesh axis runs over, the one named last changes fastest.
Arguments:
- queries: bfloat16 [4, 16, 256, 8192], P(None, 'branch', None, 'head'), may hold values from -96 to 96
- key_rows: bfloat16 [4, 16, 256, 1024], P(None, 'branch', None, 'head'), may hold values from -4 to 4
- value_rows: bfloat16 [4, 16, 256, 1024], P(None, 'branch', None, 'head'), may hold values from -5 to 5
- cotangent: bfloat16 [4, 16, 256, 8192], P(None, 'branch', None, 'head'), may hold values from -6 to 6
- out_weight: bfloat16 [8192, 8192], P('head'), may hold values from -0.0625 to 0.0625
- parents: int32 [3, 16], replicated, may hold values from 0 to 15
- seg_len: int32 [4, 16], replicated, may hold values from 128 to 256, as said below
Outputs:
- query_grad: bfloat16 [4, 16, 256, 8192], P(None, 'branch', None, 'head')
- key_grad: bfloat16 [4, 16, 256, 1024], P(None, 'branch', None, 'head')
- value_grad: bfloat16 [4, 16, 256, 1024], P(None, 'branch', None, 'head')
The draws below stay inside these ranges and needn't reach their ends.
Inputs may be any that keep to these rules, and one draw needn't show every extreme that they name: parents[m, j] is the node of level m that node j of level m + 1 continues; a node may have many children or none. `seg_len`: some node uses all 256 slots in every draw.
All inputs are finite; a program needn't handle non-finite values.
Results may differ from the reference program's by a relative error of at most 0.015.
Values may be sent and summed in bfloat16 or wider, within the bound.
No kernel may reach another device: no remote copies, remote signals or barrier semaphores. Data moves between devices by JAX's collectives and lax.ppermute only.
A program may use at most 192 MiB of HBM per device.

```python
import math
import jax
import jax.numpy as jnp
import numpy as np
from jax import lax

D = 8192
HEADS = 64
KVH = 8
HD = 128
LEVELS = 4
SEG = 256
NODES = 16


def shared_keys(key):
    sample_rows = jax.random.normal(key, (LEVELS, NODES, SEG, KVH * HD), jnp.float32)
    return jnp.clip(sample_rows, -4.0, 4.0)


def draw_key_rows(key, part):
    baseline = shared_keys(key)
    return baseline.astype(jnp.bfloat16)


def draw_queries(key, part):
    key = jax.random.fold_in(key, 5)
    sample_rows = jnp.clip(jax.random.normal(key, (LEVELS, NODES, SEG, HEADS * HD), jnp.float32), -4.0, 4.0)
    return sample_rows.astype(jnp.bfloat16)


def draw_seg_len(key, part):
    key = jax.random.fold_in(key, 9)
    first_key, second_key = jax.random.split(key)
    lengths = jax.random.randint(first_key, (LEVELS, NODES), SEG // 2, SEG + 1, jnp.int32)
    chosen = jax.random.randint(second_key, (), 0, LEVELS * NODES, jnp.int32)
    flattened = lengths.reshape(-1).at[chosen].set(SEG)
    return flattened.reshape(LEVELS, NODES).astype(jnp.int32)


def place_ends(array, stream_key, low, top_value):
    shape = array.shape
    place = [jax.random.randint(jax.random.fold_in(stream_key, axis), (), 0, shape[axis]) for axis in range(len(shape))]
    array = array.at[tuple(place)].set(low)
    longest = shape.index(max(shape))
    place[longest] = (place[longest] + 1) % shape[longest]
    return array.at[tuple(place)].set(top_value)


def level_of(own_key, dims, shards, low, high):
    level = 1.0
    for dim, blocks in shards:
        steps = jax.random.uniform(jax.random.fold_in(jax.random.fold_in(own_key, 6), dim), (blocks,), jnp.float32, low / len(shards), high / len(shards))
        level = level * jnp.repeat(jnp.exp(steps), dims[dim] // blocks).reshape((-1,) + (1,) * (len(dims) - 1 - dim))
    return level


def cumulative_ranks(amount, slope):
    weights = [(1 << 20) // math.isqrt(grade ** slope) + 1 for grade in range(1, amount + 1)]
    scale = 1 + sum(weights) // (1 << 30)
    return np.cumsum(np.array([max(1, weight // scale) for weight in weights]))


def skewed_ids(rng, dims, count, lean):
    table = cumulative_ranks(count, lean)
    pick = jax.random.randint(jax.random.fold_in(rng, 1), dims, 0, int(table[count - 1]))
    rank = jnp.searchsorted(jnp.asarray(table, jnp.int32), pick, side="right")
    return jax.random.permutation(jax.random.fold_in(rng, 2), count)[rank].astype(jnp.int32)


def normal_values(rng, shape, spread, reach, pieces=(), kind=jnp.bfloat16):
    loudness = level_of(rng, shape, pieces, -0.22, 0.18) if pieces else 1.0
    entries = jax.random.normal(rng, shape, jnp.float32) * spread * loudness
    return jnp.minimum(jnp.maximum(entries, -reach), reach).astype(kind)


def setup_inputs(seed: int = 0) -> dict:
    seeds = jax.random.split(jax.random.key(seed), 8)
    return {
        "queries": draw_queries(jax.random.fold_in(seeds[7], 71), 0),
        "key_rows": draw_key_rows(jax.random.fold_in(seeds[7], 71), 0),
        "value_rows": normal_values(seeds[2], (LEVELS, NODES, SEG, KVH * HD), 1.0, 5.0, ((1, 16), (3, 8))),
        "cotangent": normal_values(seeds[3], (LEVELS, NODES, SEG, D), 1.0, 6.0, ((1, 16), (3, 8))),
        "out_weight": normal_values(seeds[4], (HEADS * HD, D), D ** -0.5, 0.0625, ((0, 8),)),
        "parents": place_ends(skewed_ids(seeds[5], (LEVELS - 1, NODES), NODES, 2), jax.random.fold_in(seeds[5], 3), 0, NODES - 1).astype(jnp.int32),
        "seg_len": draw_seg_len(jax.random.fold_in(seeds[7], 71), 0),
    }


masked_score = -1e30


def lineage_of(parents, level_index):
    node_count = parents.shape[1]
    lineage = [None] * (level_index + 1)
    lineage[level_index] = jnp.arange(node_count, dtype=jnp.int32)
    for ancestor_level in reversed(range(level_index)):
        lineage[ancestor_level] = parents[ancestor_level][lineage[ancestor_level + 1]].astype(jnp.int32)
    return lineage


def rounded(array_in):
    narrow = lax.optimization_barrier(array_in.astype(jnp.bfloat16))
    return narrow.astype(jnp.float32)


def reference(queries, key_rows, value_rows, cotangent, out_weight, parents, seg_len):
    levels, node_count, seg_rows, q_width = queries.shape
    group_size = HEADS // KVH
    logit_scale = 1.0 / (HD ** 0.5)
    dout = jnp.dot(cotangent.reshape(-1, D), out_weight.T, preferred_element_type=jnp.float32)
    dout = dout.astype(jnp.bfloat16).reshape(levels, node_count, seg_rows, KVH, group_size, HD)
    positions = jnp.arange(seg_rows)
    query_mask = positions[None, None, :] < seg_len[:, :, None]
    dout = jnp.where(query_mask[:, :, :, None, None, None], dout, jnp.zeros_like(dout))
    query_split = queries.reshape(levels, node_count, seg_rows, KVH, group_size, HD)
    key_split = key_rows.reshape(levels, node_count, seg_rows, KVH, HD)
    value_split = value_rows.reshape(levels, node_count, seg_rows, KVH, HD)
    key_total = jnp.zeros((levels, node_count, seg_rows, KVH, HD), jnp.float32)
    value_total = jnp.zeros((levels, node_count, seg_rows, KVH, HD), jnp.float32)
    query_levels = []
    for level_index in range(levels):
        lineage = lineage_of(parents, level_index)
        key_cat = jnp.concatenate([key_split[m][lineage[m]] for m in range(level_index + 1)], axis=1)
        value_cat = jnp.concatenate([value_split[m][lineage[m]] for m in range(level_index + 1)], axis=1)
        allowed_blocks = []
        for ancestor_level in range(level_index):
            length = seg_len[ancestor_level][lineage[ancestor_level]]
            allowed_blocks.append(jnp.broadcast_to((positions[None, None, :] < length[:, None, None]), (node_count, seg_rows, seg_rows)))
        own_length = seg_len[level_index]
        own_allowed = (positions[None, None, :] <= positions[None, :, None]) & (positions[None, None, :] < own_length[:, None, None])
        allowed_blocks.append(own_allowed)
        allowed = jnp.concatenate(allowed_blocks, axis=2)

        def one_head(operands):
            query_head, key_head, value_head, dout_head = operands
            query_wide = query_head.astype(jnp.float32)
            key_wide = key_head.astype(jnp.float32)
            value_wide = value_head.astype(jnp.float32)
            output_gradient_wide = dout_head.astype(jnp.float32)
            score_matrix = jnp.einsum('surf,stf->srut', query_wide, key_wide) * logit_scale
            score_matrix = jnp.where(allowed[:, None], score_matrix, masked_score)
            maximum = jnp.max(score_matrix, axis=-1, keepdims=True)
            exponent = jnp.exp(score_matrix - maximum)
            softmax = exponent / jnp.sum(exponent, axis=-1, keepdims=True)
            probability_narrow = rounded(softmax)
            attention_weights = jnp.einsum('noha,naf->nhof', probability_narrow, value_wide)
            delta_rows = jnp.sum(output_gradient_wide * attention_weights, axis=-1)
            probability_gradient = jnp.einsum('surf,stf->srut', output_gradient_wide, value_wide)
            dscores = softmax * (probability_gradient - jnp.transpose(delta_rows, (0, 2, 1))[..., None])
            score_gradient_narrow = rounded(dscores)
            query_portion = jnp.einsum('noha,naf->nhof', score_gradient_narrow, key_wide) * logit_scale
            key_portion = jnp.einsum('fiuh,fuip->fhp', score_gradient_narrow, query_wide) * logit_scale
            value_portion = jnp.einsum('fiuh,fuip->fhp', probability_narrow, output_gradient_wide)
            return query_portion, key_portion, value_portion

        operands = (jnp.moveaxis(query_split[level_index], 2, 0), jnp.moveaxis(key_cat, 2, 0),
                    jnp.moveaxis(value_cat, 2, 0), jnp.moveaxis(dout[level_index], 2, 0))
        query_portion, key_portion, value_portion = lax.map(one_head, operands)
        query_levels.append(jnp.moveaxis(query_portion, 0, 2).astype(jnp.bfloat16).reshape(node_count, seg_rows, q_width))
        key_portion = jnp.moveaxis(key_portion, 0, 2)
        value_portion = jnp.moveaxis(value_portion, 0, 2)
        for ancestor_level in range(level_index + 1):
            start = ancestor_level * seg_rows
            key_total = key_total.at[ancestor_level, lineage[ancestor_level]].add(key_portion[:, start:start + seg_rows])
            value_total = value_total.at[ancestor_level, lineage[ancestor_level]].add(value_portion[:, start:start + seg_rows])
    query_grad = jnp.stack(query_levels, axis=0)
    key_grad = key_total.astype(jnp.bfloat16).reshape(levels, node_count, seg_rows, KVH * HD)
    value_grad = value_total.astype(jnp.bfloat16).reshape(levels, node_count, seg_rows, KVH * HD)
    return (query_grad, key_grad, value_grad)
```

```python
import functools

import jax
import jax.numpy as jnp
from jax import lax
from jax.experimental import pallas as pl
from jax.experimental.pallas import tpu as pltpu
from jax.sharding import Mesh, PartitionSpec as P

HD = 128
SEG = 256
GROUP = 8
LEVELS = 4
NODES = 16
FEATURES = 1024
HALF = 4096
PIECE = 128
SCALE = 1.0 / HD**0.5
MASKED = -1e30
NT = (((1,), (1,)), ((), ()))
AXES = ("zh", "x", "c")
ALT = [(0, 3), (1, 2), (2, 1), (3, 0)]
SWAP = [(0, 1), (1, 0)]
UP = [(i, (i + 1) % 4) for i in range(4)]
DOWN = [(i, (i + 3) % 4) for i in range(4)]


def cost(flops, size, exps=0):
    return pl.CostEstimate(flops=flops, bytes_accessed=size, transcendentals=exps)


def node_id(meta):
    return (meta[0] * 4 + meta[1]) * 2 + meta[2]


def ancestor(parents, node, level, target):
    for m in reversed(range(target, level)):
        node = parents[m * NODES + node]
    return node


def relative(meta, node):
    zh = lax.rem(node // 8 + meta[0], 2)
    x = lax.rem(lax.rem(node // 2, 4) - meta[1] + 4, 4)
    c = lax.rem(lax.rem(node, 2) + meta[2], 2)
    return (c * 4 + x) * 2 + zh


def own_product_kernel(meta, cot, weight, out):
    step = pl.program_id(1)
    part = lax.dot_general(cot[0], weight[...], NT, preferred_element_type=jnp.float32)

    @pl.when(step == 0)
    def _():
        out[...] = part

    @pl.when(step > 0)
    def _():
        out[...] += part


def own_product(meta, cot, weight):
    width = weight.shape[0]
    columns = 512
    return pl.pallas_call(
        own_product_kernel,
        grid_spec=pltpu.PrefetchScalarGridSpec(
            num_scalar_prefetch=1,
            grid=(width // columns, 4),
            in_specs=[
                pl.BlockSpec((1, SEG, FEATURES), lambda n, k, meta: (k, 0, 0)),
                pl.BlockSpec((columns, FEATURES), lambda n, k, meta: (n, meta[3] * 4 + k)),
            ],
            out_specs=pl.BlockSpec((SEG, columns), lambda n, k, meta: (0, n)),
        ),
        out_shape=jax.ShapeDtypeStruct((SEG, width), jnp.float32),
        compiler_params=pltpu.CompilerParams(vmem_limit_bytes=32 * 2**20),
        cost_estimate=cost(2 * SEG * width * HALF, 2 * width * HALF + 6 * SEG * width),
        name="own_product",
    )(meta, cot, weight)


def partner_product_kernel(cot, *refs):
    pieces, out, total = refs[:8], refs[8], refs[9]
    step = pl.program_id(0)
    rows = jnp.concatenate([piece[...] for piece in pieces], axis=0)
    part = lax.dot_general(cot[0], rows, NT, preferred_element_type=jnp.float32)

    @pl.when(step == 0)
    def _():
        total[...] = part

    @pl.when(step > 0)
    def _():
        total[...] += part

    @pl.when(step == 3)
    def _():
        for p in range(8):
            out[p] = total[:, p * PIECE : (p + 1) * PIECE].astype(jnp.bfloat16)


def partner_product(cot, pieces):
    return pl.pallas_call(
        partner_product_kernel,
        grid=(4,),
        in_specs=[pl.BlockSpec((1, SEG, FEATURES), lambda k: (k, 0, 0))]
        + [pl.BlockSpec((PIECE, FEATURES), lambda k: (0, k))] * 8,
        out_specs=pl.BlockSpec((8, SEG, PIECE), lambda k: (0, 0, 0)),
        out_shape=jax.ShapeDtypeStruct((8, SEG, PIECE), jnp.bfloat16),
        scratch_shapes=[pltpu.VMEM((SEG, 8 * PIECE), jnp.float32)],
        compiler_params=pltpu.CompilerParams(vmem_limit_bytes=32 * 2**20),
        cost_estimate=cost(2 * SEG * 1024 * HALF, 2 * 1024 * HALF + 4 * SEG * 1024),
        name="partner_product",
    )(cot, *pieces)


def probs_kernel(level, meta, parents, lengths, query, own_key, *refs):
    keys, out = refs[:level], refs[level]
    me = node_id(meta)
    q = query[0, 0]
    blocks = []
    for m in range(level + 1):
        key = keys[m][0, 0, 0] if m < level else own_key[0, 0]
        s = lax.dot_general(key, q, NT, preferred_element_type=jnp.float32)
        length = lengths[m * NODES + ancestor(parents, me, level, m)]
        position = lax.broadcasted_iota(jnp.int32, (SEG, SEG), 0)
        allowed = position < length
        if m == level:
            allowed = allowed & (position <= lax.broadcasted_iota(jnp.int32, (SEG, SEG), 1))
        blocks.append(jnp.where(allowed, s, MASKED))
    top = functools.reduce(jnp.maximum, [jnp.max(s, axis=0, keepdims=True) for s in blocks])
    exps = [jnp.exp((s - top) * SCALE) for s in blocks]
    inverse = 1.0 / sum(jnp.sum(e, axis=0, keepdims=True) for e in exps)
    for m in range(level + 1):
        out[0, m * SEG : (m + 1) * SEG] = (exps[m] * inverse).astype(jnp.bfloat16)


def gathered_spec(level, target, part):
    def index(h, meta, parents, lengths):
        node = ancestor(parents, node_id(meta), level, target)
        return relative(meta, node), target, part, 0, 0

    return pl.BlockSpec((1, 1, 1, SEG, HD), index)


def probs(level, meta, parents, lengths, queries, key_rows, gathered):
    count = (level + 1) * SEG
    return pl.pallas_call(
        functools.partial(probs_kernel, level),
        grid_spec=pltpu.PrefetchScalarGridSpec(
            num_scalar_prefetch=3,
            grid=(GROUP,),
            in_specs=[
                pl.BlockSpec((1, 1, SEG, HD), lambda h, *_: (level, 0, 0, h)),
                pl.BlockSpec((1, 1, SEG, HD), lambda h, *_: (level, 0, 0, 0)),
            ]
            + [gathered_spec(level, m, 0) for m in range(level)],
            out_specs=pl.BlockSpec((1, count, SEG), lambda h, *_: (h, 0, 0)),
        ),
        out_shape=jax.ShapeDtypeStruct((GROUP, count, SEG), jnp.bfloat16),
        compiler_params=pltpu.CompilerParams(vmem_limit_bytes=32 * 2**20),
        cost_estimate=cost(
            2 * GROUP * count * SEG * HD, 2 * GROUP * count * SEG, GROUP * count * SEG
        ),
        name=f"probs_{level}",
    )(meta, parents, lengths, queries, key_rows, *[gathered] * level)


def backward_kernel(
    level, meta, parents, lengths, probs_ref, query, own, partner, own_key, own_value, *refs
):
    keys, refs = refs[:level], refs[level:]
    values, refs = refs[:level], refs[level:]
    if level:
        query_out, own_out, ancestor_out, flipped, key_total, value_total = refs
    else:
        query_out, own_out, flipped, key_total, value_total = refs
    head = pl.program_id(0)
    blocks = [slice(m * SEG, (m + 1) * SEG) for m in range(level + 1)]
    key_blocks = [keys[m][0, 0, 0] for m in range(level)] + [own_key[0, 0]]
    value_blocks = [values[m][0, 0, 0] for m in range(level)] + [own_value[0, 0]]

    @pl.when(head == 0)
    def _():
        key_total[...] = jnp.zeros_like(key_total)
        value_total[...] = jnp.zeros_like(value_total)
        for m in range(level + 1):
            flipped[:, blocks[m]] = key_blocks[m].astype(jnp.float32).T.astype(jnp.bfloat16)

    length = lengths[level * NODES + node_id(meta)]
    position = lax.broadcasted_iota(jnp.int32, (SEG, HD), 0)
    total = own[...] + partner[0].astype(jnp.float32)
    dout = jnp.where(position < length, total, 0.0).astype(jnp.bfloat16)
    q = query[0, 0]
    wide = [probs_ref[0, block].astype(jnp.float32) for block in blocks]
    grads = [
        lax.dot_general(value, dout, NT, preferred_element_type=jnp.float32)
        for value in value_blocks
    ]
    delta = sum(jnp.sum(p * g, axis=0, keepdims=True) for p, g in zip(wide, grads))
    query_total = jnp.zeros((HD, SEG), jnp.float32)
    for m in range(level + 1):
        scores = (wide[m] * (grads[m] - delta)).astype(jnp.bfloat16)
        key_total[blocks[m]] += jnp.dot(scores, q, preferred_element_type=jnp.float32)
        value_total[blocks[m]] += jnp.dot(
            probs_ref[0, blocks[m]], dout, preferred_element_type=jnp.float32
        )
        query_total += jnp.dot(
            flipped[:, blocks[m]], scores, preferred_element_type=jnp.float32
        )
    query_out[...] = (query_total * SCALE).T.astype(jnp.bfloat16)

    @pl.when(head == GROUP - 1)
    def _():
        for m in range(level):
            ancestor_out[m, 0] = (key_total[blocks[m]] * SCALE).astype(jnp.bfloat16)
            ancestor_out[m, 1] = value_total[blocks[m]].astype(jnp.bfloat16)
        own_out[0] = key_total[blocks[level]] * SCALE
        own_out[1] = value_total[blocks[level]]


def backward(
    level, meta, parents, lengths, probabilities, queries, own, partner, key_rows, value_rows, gathered
):
    count = (level + 1) * SEG
    width = GROUP * HD

    def piece_index(h, meta, *_):
        quarter = lax.rem(h // 2 - meta[1] + 4, 4)
        return lax.rem(lax.rem(h, 2) + meta[2], 2) * 4 + quarter, 0, 0

    out_specs = [
        pl.BlockSpec((SEG, HD), lambda h, *_: (0, h)),
        pl.BlockSpec((2, SEG, HD), lambda h, *_: (0, 0, 0)),
    ]
    out_shape = [
        jax.ShapeDtypeStruct((SEG, width), jnp.bfloat16),
        jax.ShapeDtypeStruct((2, SEG, HD), jnp.float32),
    ]
    if level:
        out_specs.append(pl.BlockSpec((level, 2, SEG, HD), lambda h, *_: (0, 0, 0, 0)))
        out_shape.append(jax.ShapeDtypeStruct((level, 2, SEG, HD), jnp.bfloat16))
    return pl.pallas_call(
        functools.partial(backward_kernel, level),
        grid_spec=pltpu.PrefetchScalarGridSpec(
            num_scalar_prefetch=3,
            grid=(GROUP,),
            in_specs=[
                pl.BlockSpec((1, count, SEG), lambda h, *_: (h, 0, 0)),
                pl.BlockSpec((1, 1, SEG, HD), lambda h, *_: (level, 0, 0, h)),
                pl.BlockSpec((SEG, HD), lambda h, *_: (0, h)),
                pl.BlockSpec((1, SEG, PIECE), piece_index),
                pl.BlockSpec((1, 1, SEG, HD), lambda h, *_: (level, 0, 0, 0)),
                pl.BlockSpec((1, 1, SEG, HD), lambda h, *_: (level, 0, 0, 0)),
            ]
            + [gathered_spec(level, m, 0) for m in range(level)]
            + [gathered_spec(level, m, 1) for m in range(level)],
            out_specs=out_specs,
            scratch_shapes=[
                pltpu.VMEM((HD, count), jnp.bfloat16),
                pltpu.VMEM((count, HD), jnp.float32),
                pltpu.VMEM((count, HD), jnp.float32),
            ],
        ),
        out_shape=out_shape,
        compiler_params=pltpu.CompilerParams(vmem_limit_bytes=32 * 2**20),
        cost_estimate=cost(8 * GROUP * count * SEG * HD, 2 * GROUP * count * SEG),
        name=f"backward_{level}",
    )(
        meta, parents, lengths, probabilities, queries, own, partner, key_rows, value_rows,
        *[gathered] * (2 * level),
    )


def spread_kernel(target, meta, parents, *refs):
    terms, out = refs[:-1], refs[-1]
    slot = pl.program_id(0)
    me = node_id(meta)
    sibling = me + 1 - 2 * meta[2]
    wanted = (lax.rem(slot, 2) * 4 + slot // 2) * 2 + meta[2]
    total = jnp.zeros(out.shape[1:], jnp.float32)
    count = LEVELS - 1 - target
    for i, term in enumerate(terms):
        level = target + 1 + i % count
        node = me if i < count else sibling
        hit = ancestor(parents, node, level, target) == wanted
        total += jnp.where(hit, term[0].astype(jnp.float32), 0.0)
    out[0] = total.astype(jnp.bfloat16)


def spread(target, meta, parents, terms):
    return pl.pallas_call(
        functools.partial(spread_kernel, target),
        grid_spec=pltpu.PrefetchScalarGridSpec(
            num_scalar_prefetch=2,
            grid=(8,),
            in_specs=[pl.BlockSpec((1, 2, SEG, HD), lambda n, *_: (target, 0, 0, 0))] * len(terms),
            out_specs=pl.BlockSpec((1, 2, SEG, HD), lambda n, *_: (n, 0, 0, 0)),
        ),
        out_shape=jax.ShapeDtypeStruct((8, 2, SEG, HD), jnp.bfloat16),
        compiler_params=pltpu.CompilerParams(vmem_limit_bytes=32 * 2**20),
        cost_estimate=cost(8 * len(terms) * 2 * SEG * HD, 16 * 2 * SEG * HD),
        name=f"spread_{target}",
    )(meta, parents, *terms)


def gather_rows(key_rows, value_rows):
    own = jnp.stack([key_rows[: LEVELS - 1, 0], value_rows[: LEVELS - 1, 0]], axis=1)
    pair = jnp.stack([own, lax.ppermute(own, "zh", SWAP)])
    below = lax.ppermute(pair, "x", UP)
    above = lax.ppermute(pair, "x", DOWN)
    across = jnp.stack(
        [lax.ppermute(above[0], "x", DOWN), lax.ppermute(below[1], "x", UP)]
    )
    mine = jnp.concatenate([pair, above, across, below])
    return jnp.concatenate([mine, lax.ppermute(mine, "c", SWAP)])


def partner_weight(out_weight, zh, x, c, zl):
    def rows(quarter):
        return lax.dynamic_slice(
            out_weight, (quarter * 256 + c * PIECE, (1 - zl) * HALF), (PIECE, HALF)
        )

    first = lax.ppermute(rows(x), "zl", SWAP)
    second = lax.ppermute(rows(lax.rem(x + 1, 4)), ("zh", "zl"), ALT)
    third = lax.ppermute(second, "x", DOWN)
    fourth = lax.ppermute(first, "x", UP)
    mine = [first, second, third, fourth]
    return mine + [lax.ppermute(piece, "c", SWAP) for piece in mine]


def local(queries, key_rows, value_rows, cotangent, out_weight, parents, seg_len):
    zh, x, c, zl, y = [lax.axis_index(name) for name in ("zh", "x", "c", "zl", "y")]
    meta = jnp.stack([zh, x, c, zl, y]).astype(jnp.int32)
    parents = parents.reshape(-1)
    lengths = seg_len.reshape(-1)
    cots = [None] * LEVELS
    for level in reversed(range(LEVELS)):
        cots[level] = lax.all_gather(cotangent[level, 0], "y")
    weights = partner_weight(out_weight, zh, x, c, zl)
    gathered = gather_rows(key_rows, value_rows)
    query_grads = [None] * LEVELS
    own_grads = [None] * LEVELS
    terms = [None] * LEVELS
    passed = [None] * LEVELS
    sums = [None] * LEVELS
    for level in reversed(range(LEVELS)):
        partner = lax.ppermute(partner_product(cots[level], weights), "zl", SWAP)
        own = own_product(meta, cots[level], out_weight)
        probabilities = probs(level, meta, parents, lengths, queries, key_rows, gathered)
        results = backward(
            level, meta, parents, lengths, probabilities, queries, own, partner,
            key_rows, value_rows, gathered,
        )
        query_grads[level], own_grads[level] = results[:2]
        if level:
            terms[level] = results[2]
            passed[level] = lax.ppermute(results[2], "c", SWAP)
            target = level - 1
            dense = spread(target, meta, parents, terms[level:] + passed[level:])
            part = lax.psum_scatter(
                dense.reshape(4, 2, 2, SEG, HD), "x", scatter_dimension=0, tiled=False
            )
            kept = lax.dynamic_index_in_dim(part, zh, 0, keepdims=False)
            given = lax.dynamic_index_in_dim(part, 1 - zh, 0, keepdims=False)
            sums[target] = (kept, lax.ppermute(given, "zh", SWAP))
    finals = [
        (own_grads[t] + sums[t][0].astype(jnp.float32) + sums[t][1].astype(jnp.float32))
        for t in range(LEVELS - 1)
    ] + [own_grads[LEVELS - 1]]
    query_grad = jnp.stack(query_grads)[:, None]
    key_grad = jnp.stack([f[0] for f in finals])[:, None].astype(jnp.bfloat16)
    value_grad = jnp.stack([f[1] for f in finals])[:, None].astype(jnp.bfloat16)
    return (query_grad, key_grad, value_grad)


def solution(mesh):
    fine = Mesh(mesh.devices.reshape(2, 4, 2, 2, 4), ("zh", "x", "c", "zl", "y"))
    rows = P(None, AXES, None, ("zl", "y"))
    in_specs = (rows, rows, rows, rows, P(("zl", "y"), None), P(), P())
    return jax.shard_map(
        local, mesh=fine, in_specs=in_specs, out_specs=(rows, rows, rows), check_vma=False
    )
```

```python
import functools

import jax
import jax.numpy as jnp
from jax import lax
from jax.experimental import pallas as pl
from jax.experimental.pallas import tpu as pltpu
from jax.sharding import Mesh, PartitionSpec as P

HD = 128
SEG = 256
GROUP = 8
BATCH = 4
LEVELS = 4
NODES = 16
FEATURES = 1024
HALF = 4096
PIECE = 128
SCALE = 1.0 / HD**0.5
EXP2_SCALE = SCALE * 1.4426950408889634
MASKED = -1e30
NT = (((1,), (1,)), ((), ()))
PARAMS = pltpu.CompilerParams(vmem_limit_bytes=56 * 2**20)
ANY = pl.BlockSpec(memory_space=pl.ANY)
AXES = ("zh", "x", "c")
ALT = [(0, 3), (1, 2), (2, 1), (3, 0)]
SWAP = [(0, 1), (1, 0)]
UP = [(i, (i + 1) % 4) for i in range(4)]
DOWN = [(i, (i + 3) % 4) for i in range(4)]
ACROSS = [(i, (i + 2) % 4) for i in range(4)]


def cost(flops, size, exps=0):
    return pl.CostEstimate(flops=flops, bytes_accessed=size, transcendentals=exps)


def node_id(meta):
    return (meta[0] * 4 + meta[1]) * 2 + meta[2]


def ancestor(parents, node, level, target):
    for m in reversed(range(target, level)):
        node = parents[m * NODES + node]
    return node


def relative(meta, node):
    zh = lax.rem(node // 8 + meta[0], 2)
    x = lax.rem(node // 2, 4)
    c = lax.rem(lax.rem(node, 2) + meta[2], 2)
    return c, x, zh


def prepare_kernel(meta, weight, keys, values, cot, first, second, rows, upper, lower, *refs):
    held, kept, passed, in_sems, out_sems = refs

    def piece(step):
        row = pl.multiple_of(lax.rem(meta[1] + step, 4) * 256 + meta[2] * PIECE, PIECE)
        column = pl.multiple_of((1 - meta[3]) * HALF, HALF)
        return weight.at[pl.ds(row, PIECE), pl.ds(column, HALF)]

    moves = [
        (piece(0), held.at[0], first),
        (piece(1), held.at[1], second),
        (cot.at[2:4, 0], passed.at[0], upper),
        (cot.at[0:2, 0], passed.at[1], lower),
        (keys.at[0 : LEVELS - 1, 0], kept.at[0], rows.at[0]),
        (values.at[0 : LEVELS - 1, 0], kept.at[1], rows.at[1]),
    ]
    reads = [
        pltpu.make_async_copy(source, middle, in_sems.at[i])
        for i, (source, middle, _) in enumerate(moves)
    ]
    writes = [
        pltpu.make_async_copy(middle, target, out_sems.at[i])
        for i, (_, middle, target) in enumerate(moves)
    ]
    for read in reads:
        read.start()
    for read, write in zip(reads, writes):
        read.wait()
        write.start()
    for write in writes:
        write.wait()


def prepare(meta, weight, keys, values, cot):
    return pl.pallas_call(
        prepare_kernel,
        grid_spec=pltpu.PrefetchScalarGridSpec(
            num_scalar_prefetch=1,
            grid=(),
            in_specs=[ANY] * 4,
            out_specs=[ANY] * 5,
            scratch_shapes=[
                pltpu.VMEM((2, PIECE, HALF), jnp.bfloat16),
                pltpu.VMEM((2, LEVELS - 1, SEG, HD), jnp.bfloat16),
                pltpu.VMEM((2, 2, SEG, FEATURES), jnp.bfloat16),
                pltpu.SemaphoreType.DMA((6,)),
                pltpu.SemaphoreType.DMA((6,)),
            ],
        ),
        out_shape=[
            jax.ShapeDtypeStruct((PIECE, HALF), jnp.bfloat16),
            jax.ShapeDtypeStruct((PIECE, HALF), jnp.bfloat16),
            jax.ShapeDtypeStruct((2, LEVELS - 1, SEG, HD), jnp.bfloat16),
            jax.ShapeDtypeStruct((2, SEG, FEATURES), jnp.bfloat16),
            jax.ShapeDtypeStruct((2, SEG, FEATURES), jnp.bfloat16),
        ],
        compiler_params=PARAMS,
        cost_estimate=cost(0, 12 * 2**20),
        name="prepare",
    )(meta, weight, keys, values, cot)


def product_kernel(partner, meta, own, above, below, first, second, *refs):
    count = 8 if partner else 1
    weights, refs = refs[:count], refs[count:]
    outs, (cots, held, cot_sems, sems) = refs[1:-4], refs[-4:]
    copies = []

    def copy(source, target, sem):
        made = pltpu.make_async_copy(source, target, sem)
        made.start()
        return made

    def block(q):
        if partner:
            return [
                copy(weights[q], held.at[q, 0:PIECE], sems.at[q, 0]),
                copy(weights[4 + q], held.at[q, PIECE : 2 * PIECE], sems.at[q, 1]),
            ]
        column = pl.multiple_of(meta[3] * HALF, HALF)
        source = weights[0].at[q * 256 : (q + 1) * 256, pl.ds(column, HALF)]
        return [copy(source, held.at[q], sems.at[q, 0])]

    def place(source, step, sem, *index):
        column = pl.multiple_of(lax.rem(meta[4] + step, 4) * FEATURES, FEATURES)
        target = cots.at[(*(index or (slice(None),)), slice(None), pl.ds(column, FEATURES))]
        return copy(source, target, cot_sems.at[sem])

    waits = [
        place(own, 0, 0),
        place(above, 1, 1),
        place(below, 3, 2),
        place(first, 2, 3, 0),
        place(second, 2, 4, 1),
    ]
    copies = [block(q) for q in range(4)]
    for q in range(4):
        for made in (waits if q == 0 else []) + copies[q]:
            made.wait()
        total = lax.dot_general(
            cots[...].reshape(2 * SEG, HALF), held[q], NT, preferred_element_type=jnp.float32
        )
        for i in range(2):
            part = total[i * SEG : (i + 1) * SEG]
            if partner:
                outs[i][q] = part[:, :PIECE].astype(jnp.bfloat16)
                outs[i][4 + q] = part[:, PIECE:].astype(jnp.bfloat16)
            else:
                outs[i][:, q * 256 : (q + 1) * 256] = part


def product(partner, meta, cots, weights, token):
    if partner:
        out_shape = [jax.ShapeDtypeStruct((8, SEG, PIECE), jnp.bfloat16)] * 2
    else:
        out_shape = [jax.ShapeDtypeStruct((SEG, FEATURES), jnp.float32)] * 2
    return pl.pallas_call(
        functools.partial(product_kernel, partner),
        grid_spec=pltpu.PrefetchScalarGridSpec(
            num_scalar_prefetch=1,
            grid=(),
            in_specs=[ANY] * (6 + len(weights)),
            out_specs=[pl.BlockSpec(memory_space=pltpu.VMEM)] * 2,
            scratch_shapes=[
                pltpu.VMEM((2, SEG, HALF), jnp.bfloat16),
                pltpu.VMEM((4, 256, HALF), jnp.bfloat16),
                pltpu.SemaphoreType.DMA((5,)),
                pltpu.SemaphoreType.DMA((4, 2)),
            ],
        ),
        out_shape=out_shape,
        compiler_params=PARAMS,
        cost_estimate=cost(4 * SEG * 1024 * HALF, 2 * 1024 * HALF + 8 * SEG * 1024),
        name="partner_product" if partner else "own_product",
    )(meta, *cots, *weights, token)


def pair_index(level, target):
    return level * (level - 1) // 2 + target


PAIRS = [(level, m) for level in range(LEVELS) for m in range(level)]


def probs_kernel(meta, parents, lengths, query, own_key, mine, other, *refs):
    outs, picked, sems = refs[1:5], refs[5], refs[6]
    me = node_id(meta)

    @pl.when(pl.program_id(0) == 0)
    def _():
        copies = []
        for i, (level, m) in enumerate(PAIRS):
            c, x, zh = relative(meta, ancestor(parents, me, level, m))
            for part in range(2):
                pair = [
                    pltpu.make_async_copy(
                        source.at[x, zh, part, m], picked.at[i, part], sems.at[i, part]
                    )
                    for source in (mine, other)
                ]
                pl.when(c == 0)(pair[0].start)
                pl.when(c == 1)(pair[1].start)
                copies.append(pair[0])
        for copy in copies:
            copy.wait()

    for level in reversed(range(LEVELS)):
        q = jnp.concatenate(
            [query[level, 0, :, i * HD : (i + 1) * HD] for i in range(BATCH)], axis=0
        )
        blocks = []
        for m in range(level + 1):
            key = picked[pair_index(level, m), 0] if m < level else own_key[level, 0]
            s = lax.dot_general(key, q, NT, preferred_element_type=jnp.float32)
            length = lengths[m * NODES + ancestor(parents, me, level, m)]
            position = lax.broadcasted_iota(jnp.int32, s.shape, 0)
            allowed = position < length
            if m == level:
                asked = lax.broadcasted_iota(jnp.int32, s.shape, 1) & (SEG - 1)
                allowed = allowed & (position <= asked)
            blocks.append(jnp.where(allowed, s, MASKED))
        top = functools.reduce(
            jnp.maximum, [jnp.max(s, axis=0, keepdims=True) for s in blocks]
        )
        exps = [jnp.exp2((s - top) * EXP2_SCALE) for s in blocks]
        inverse = 1.0 / sum(jnp.sum(e, axis=0, keepdims=True) for e in exps)
        for m in range(level + 1):
            outs[level][0, m * SEG : (m + 1) * SEG] = (exps[m] * inverse).astype(jnp.bfloat16)


def probs(meta, parents, lengths, queries, key_rows, mine, other, token):
    width = BATCH * HD
    counts = [(level + 1) * SEG for level in range(LEVELS)]
    total = sum(counts)
    return pl.pallas_call(
        probs_kernel,
        grid_spec=pltpu.PrefetchScalarGridSpec(
            num_scalar_prefetch=3,
            grid=(GROUP // BATCH,),
            in_specs=[
                pl.BlockSpec((LEVELS, 1, SEG, width), lambda h, *_: (0, 0, 0, h)),
                pl.BlockSpec((LEVELS, 1, SEG, HD), lambda h, *_: (0, 0, 0, 0)),
                ANY,
                ANY,
                ANY,
            ],
            out_specs=[
                pl.BlockSpec((1, count, BATCH * SEG), lambda h, *_: (h, 0, 0))
                for count in counts
            ]
            + [pl.BlockSpec((len(PAIRS), 2, SEG, HD), lambda h, *_: (0, 0, 0, 0))],
            scratch_shapes=[pltpu.SemaphoreType.DMA((len(PAIRS), 2))],
        ),
        out_shape=[
            jax.ShapeDtypeStruct((GROUP // BATCH, count, BATCH * SEG), jnp.bfloat16)
            for count in counts
        ]
        + [jax.ShapeDtypeStruct((len(PAIRS), 2, SEG, HD), jnp.bfloat16)],
        compiler_params=PARAMS,
        cost_estimate=cost(
            2 * GROUP * total * SEG * HD, 2 * GROUP * total * SEG, GROUP * total * SEG
        ),
        name="probs",
    )(meta, parents, lengths, queries, key_rows, mine, other, token)


def backward_kernel(
    level, meta, parents, lengths, probs_ref, query, own, partner, own_key, own_value, *refs
):
    if level:
        picked, refs = refs[0], refs[1:]
    refs = refs[1:]
    if level:
        query_out, own_out, kept_out, given_out, flipped, key_total, value_total = refs
    else:
        query_out, own_out, flipped, key_total, value_total = refs
    first = pair_index(level, 0)
    step = pl.program_id(0)
    blocks = [slice(m * SEG, (m + 1) * SEG) for m in range(level + 1)]

    @pl.when(step == 0)
    def _():
        key_total[...] = jnp.zeros_like(key_total)
        value_total[...] = jnp.zeros_like(value_total)
        for m in range(level + 1):
            key = picked[first + m, 0] if m < level else own_key[0, 0]
            flipped[:, blocks[m]] = key.astype(jnp.float32).T.astype(jnp.bfloat16)

    length = lengths[level * NODES + node_id(meta)]
    valid = lax.broadcasted_iota(jnp.int32, (SEG, HD), 0) < length
    heads = []
    for i in range(BATCH):
        head = step * BATCH + i
        piece = lax.rem(head + meta[2], 2) * 4 + lax.rem(head // 2 - meta[1] + 4, 4)
        total = own[:, i * HD : (i + 1) * HD] + partner[piece].astype(jnp.float32)
        heads.append(jnp.where(valid, total, 0.0).astype(jnp.bfloat16))
    dout = jnp.concatenate(heads, axis=0)
    q = jnp.concatenate([query[0, 0, :, i * HD : (i + 1) * HD] for i in range(BATCH)], axis=0)
    value = jnp.concatenate(
        [picked[first + m, 1] for m in range(level)] + [own_value[0, 0]], axis=0
    )
    narrow = probs_ref[0]
    wide = narrow.astype(jnp.float32)
    grads = lax.dot_general(value, dout, NT, preferred_element_type=jnp.float32)
    delta = jnp.sum(wide * grads, axis=0, keepdims=True)
    scores = (wide * (grads - delta)).astype(jnp.bfloat16)
    key_total[...] += jnp.dot(scores, q, preferred_element_type=jnp.float32)
    value_total[...] += jnp.dot(narrow, dout, preferred_element_type=jnp.float32)
    query_total = jnp.dot(flipped[...], scores, preferred_element_type=jnp.float32) * SCALE
    for i in range(BATCH):
        part = query_total[:, i * SEG : (i + 1) * SEG]
        query_out[0, 0, :, i * HD : (i + 1) * HD] = part.T.astype(jnp.bfloat16)

    @pl.when(step == GROUP // BATCH - 1)
    def _():
        for m in range(level):
            key_part = (key_total[blocks[m]] * SCALE).astype(jnp.bfloat16)
            value_part = value_total[blocks[m]].astype(jnp.bfloat16)
            keep_key = meta[2] == 0
            kept_out[m] = jnp.where(keep_key, key_part, value_part)
            given_out[m] = jnp.where(keep_key, value_part, key_part)
        own_out[0] = key_total[blocks[level]] * SCALE
        own_out[1] = value_total[blocks[level]]


def backward(
    level, meta, parents, lengths, probabilities, queries, own, partner, key_rows, value_rows,
    picked, token,
):
    count = (level + 1) * SEG
    width = BATCH * HD
    out_specs = [
        pl.BlockSpec((1, 1, SEG, width), lambda h, *_: (level, 0, 0, h)),
        pl.BlockSpec((2, SEG, HD), lambda h, *_: (0, 0, 0)),
    ]
    out_shape = [
        jax.ShapeDtypeStruct(queries.shape, jnp.bfloat16),
        jax.ShapeDtypeStruct((2, SEG, HD), jnp.float32),
    ]
    if level:
        out_specs += [pl.BlockSpec((level, SEG, HD), lambda h, *_: (0, 0, 0))] * 2
        out_shape += [jax.ShapeDtypeStruct((level, SEG, HD), jnp.bfloat16)] * 2
    last = level == LEVELS - 1
    return pl.pallas_call(
        functools.partial(backward_kernel, level),
        grid_spec=pltpu.PrefetchScalarGridSpec(
            num_scalar_prefetch=3,
            grid=(GROUP // BATCH,),
            in_specs=[
                pl.BlockSpec((1, count, BATCH * SEG), lambda h, *_: (h, 0, 0)),
                pl.BlockSpec((1, 1, SEG, width), lambda h, *_: (level, 0, 0, h)),
                pl.BlockSpec((SEG, width), lambda h, *_: (0, h)),
                pl.BlockSpec((8, SEG, PIECE), lambda h, *_: (0, 0, 0)),
                pl.BlockSpec((1, 1, SEG, HD), lambda h, *_: (level, 0, 0, 0)),
                pl.BlockSpec((1, 1, SEG, HD), lambda h, *_: (level, 0, 0, 0)),
            ]
            + [pl.BlockSpec((len(PAIRS), 2, SEG, HD), lambda h, *_: (0, 0, 0, 0))] * min(level, 1)
            + [ANY],
            out_specs=out_specs,
            scratch_shapes=[
                pltpu.VMEM((HD, count), jnp.bfloat16),
                pltpu.VMEM((count, HD), jnp.float32),
                pltpu.VMEM((count, HD), jnp.float32),
            ],
        ),
        out_shape=out_shape,
        input_output_aliases={} if last else {10 if level else 9: 0},
        compiler_params=PARAMS,
        cost_estimate=cost(8 * GROUP * count * SEG * HD, 2 * GROUP * count * SEG),
        name=f"backward_{level}",
    )(
        meta, parents, lengths, probabilities, queries, own, partner, key_rows, value_rows,
        *[picked] * min(level, 1), token,
    )


def spread_kernel(target, meta, parents, *refs):
    terms, outs = refs[:-4], refs[-4:]
    me = node_id(meta)
    sibling = me + 1 - 2 * meta[2]
    other = 8 - 16 * meta[0]
    places = []
    blocks = []
    for i, pair in enumerate(terms):
        level = target + 1 + i // 2
        away = other if i % 2 else 0
        for j, node in enumerate((me + away, sibling + away)):
            places.append(ancestor(parents, node, level, target))
            blocks.append(pair[j, 0])
    for step, out in enumerate(outs):
        x = lax.rem(meta[1] + step, 4)
        for c in range(2):
            wanted = (meta[0] * 4 + x) * 2 + c
            total = jnp.zeros((SEG, HD), jnp.float32)
            for block, place in zip(blocks, places):
                total += jnp.where(place == wanted, block.astype(jnp.float32), 0.0)
            out[c] = total.astype(jnp.bfloat16)


def spread(target, meta, parents, terms):
    return pl.pallas_call(
        functools.partial(spread_kernel, target),
        grid_spec=pltpu.PrefetchScalarGridSpec(
            num_scalar_prefetch=2,
            grid=(1,),
            in_specs=[pl.BlockSpec((2, 1, SEG, HD), lambda n, *_: (0, target, 0, 0))] * len(terms),
            out_specs=[pl.BlockSpec((2, SEG, HD), lambda n, *_: (0, 0, 0))] * 4,
        ),
        out_shape=[jax.ShapeDtypeStruct((2, SEG, HD), jnp.bfloat16)] * 4,
        compiler_params=PARAMS,
        cost_estimate=cost(8 * len(terms) * 2 * SEG * HD, 16 * 2 * SEG * HD),
        name=f"spread_{target}",
    )(meta, parents, *terms)


def collect_kernel(meta, *refs):
    parts, (kept, given) = refs[:4], refs[4:]
    kept[...] = sum(part[meta[2]].astype(jnp.float32) for part in parts)
    given[...] = sum(part[1 - meta[2]].astype(jnp.float32) for part in parts)


def collect(meta, parts):
    whole = pl.BlockSpec((2, SEG, HD), lambda n, *_: (0, 0, 0))
    return pl.pallas_call(
        collect_kernel,
        grid_spec=pltpu.PrefetchScalarGridSpec(
            num_scalar_prefetch=1,
            grid=(1,),
            in_specs=[whole] * 4,
            out_specs=[pl.BlockSpec((SEG, HD), lambda n, *_: (0, 0))] * 2,
        ),
        out_shape=[jax.ShapeDtypeStruct((SEG, HD), jnp.float32)] * 2,
        compiler_params=PARAMS,
        cost_estimate=cost(8 * SEG * HD, 24 * SEG * HD),
        name="collect",
    )(meta, *parts)


def finish_kernel(meta, *refs):
    owns, kept, given, outs = refs[:LEVELS], refs[LEVELS:7], refs[7:10], refs[10:]
    keep_key = meta[2] == 0
    for t in range(LEVELS):
        for part in range(2):
            total = owns[t][part]
            if t < LEVELS - 1:
                mine = keep_key if part == 0 else jnp.logical_not(keep_key)
                total += jnp.where(mine, kept[t][...], given[t][...])
            outs[part][t, 0] = total.astype(jnp.bfloat16)


def finish(meta, owns, kept, given, shape):
    one = pl.BlockSpec((SEG, HD), lambda n, *_: (0, 0))
    both = pl.BlockSpec((2, SEG, HD), lambda n, *_: (0, 0, 0))
    return pl.pallas_call(
        finish_kernel,
        grid_spec=pltpu.PrefetchScalarGridSpec(
            num_scalar_prefetch=1,
            grid=(1,),
            in_specs=[both] * LEVELS + [one] * 6,
            out_specs=[pl.BlockSpec((LEVELS, 1, SEG, HD), lambda n, *_: (0, 0, 0, 0))] * 2,
        ),
        out_shape=[jax.ShapeDtypeStruct(shape, jnp.bfloat16)] * 2,
        compiler_params=PARAMS,
        cost_estimate=cost(16 * SEG * HD, 64 * SEG * HD),
        name="finish",
    )(meta, *owns, *kept, *given)


def gather_rows(own):
    pair = jnp.stack([own, lax.ppermute(own, "zh", SWAP)])
    mine = lax.all_gather(pair, "x")
    return mine, lax.ppermute(mine, "c", SWAP)


def gather_cotangent(pair):
    above = lax.ppermute(pair, "y", DOWN)
    below = lax.ppermute(pair, "y", UP)
    first = lax.ppermute(above[0], "y", DOWN)
    second = lax.ppermute(below[1], "y", UP)
    return pair, above, below, first, second


def partner_weight(first, second):
    first = lax.ppermute(first, "zl", SWAP)
    second = lax.ppermute(second, ("zh", "zl"), ALT)
    third = lax.ppermute(second, "x", DOWN)
    fourth = lax.ppermute(first, "x", UP)
    mine = [first, second, third, fourth]
    return mine + [lax.ppermute(piece, "c", SWAP) for piece in mine]


def local(queries, key_rows, value_rows, cotangent, out_weight, parents, seg_len):
    zh, x, c, zl, y = [lax.axis_index(name) for name in ("zh", "x", "c", "zl", "y")]
    meta = jnp.stack([zh, x, c, zl, y]).astype(jnp.int32)
    parents = parents.reshape(-1)
    lengths = seg_len.reshape(-1)
    first, second, rows, upper, lower = prepare(
        meta, out_weight, key_rows, value_rows, cotangent
    )
    weights = partner_weight(first, second)
    cots = [gather_cotangent(lower), gather_cotangent(upper)]
    mine, other = gather_rows(rows)
    table = (meta, parents, lengths)
    owns = [None] * LEVELS
    partners = [None] * LEVELS

    def own_pair(i, token):
        owns[2 * i], owns[2 * i + 1] = product(False, meta, cots[i], [out_weight], token)
        return owns[2 * i]

    def partner_pair(i, token):
        parts = product(True, meta, cots[i], weights, token)
        for j in (1, 0):
            partners[2 * i + j] = lax.ppermute(parts[j], "zl", SWAP)
        return parts[0]

    token = own_pair(1, meta)
    token = partner_pair(1, token)
    *probabilities, picked = probs(*table, queries, key_rows, mine, other, token)
    token = partner_pair(0, picked)
    query_grad = own_pair(0, token)
    own_grads = [None] * LEVELS
    terms = []
    kept = [None] * (LEVELS - 1)
    given = [None] * (LEVELS - 1)
    for level in reversed(range(LEVELS)):
        query_grad, own_grads[level], *rest = backward(
            level, *table, probabilities[level], queries, owns[level], partners[level],
            key_rows, value_rows, picked, query_grad,
        )
        if level:
            target = level - 1
            near = jnp.stack([rest[0], lax.ppermute(rest[1], "c", SWAP)])
            terms = [near, lax.ppermute(near, "zh", SWAP)] + terms
            here, up, across, down = spread(target, meta, parents, terms)
            parts = [
                here,
                lax.ppermute(up, "x", UP),
                lax.ppermute(down, "x", DOWN),
                lax.ppermute(across, "x", ACROSS),
            ]
            kept[target], give = collect(meta, parts)
            given[target] = lax.ppermute(give, "c", SWAP)
    key_grad, value_grad = finish(meta, own_grads, kept, given, key_rows.shape)
    return (query_grad, key_grad, value_grad)


def solution(mesh):
    fine = Mesh(mesh.devices.reshape(2, 4, 2, 2, 4), ("zh", "x", "c", "zl", "y"))
    rows = P(None, AXES, None, ("zl", "y"))
    in_specs = (rows, rows, rows, rows, P(("zl", "y"), None), P(), P())
    return jax.shard_map(
        local, mesh=fine, in_specs=in_specs, out_specs=(rows, rows, rows), check_vma=False
    )
```

```python
import functools

import jax
import jax.numpy as jnp
from jax import lax
from jax.experimental import pallas as pl
from jax.experimental.pallas import tpu as pltpu
from jax.sharding import Mesh, PartitionSpec as P

HD = 128
SEG = 256
GROUP = 8
BATCH = 4
LEVELS = 4
NODES = 16
FEATURES = 1024
HALF = 4096
PIECE = 128
ROWS = 256
SCALE = 1.0 / HD**0.5
EXP2_SCALE = SCALE * 1.4426950408889634
MASKED = -1e30
NT = (((1,), (1,)), ((), ()))
PARAMS = pltpu.CompilerParams(vmem_limit_bytes=56 * 2**20)
SMALL = pltpu.CompilerParams(vmem_limit_bytes=16 * 2**20)
ANY = pl.BlockSpec(memory_space=pl.ANY)
AXES = ("zh", "x", "c")
ALT = [(0, 3), (1, 2), (2, 1), (3, 0)]
SWAP = [(0, 1), (1, 0)]
UP = [(i, (i + 1) % 4) for i in range(4)]
DOWN = [(i, (i + 3) % 4) for i in range(4)]
ACROSS = [(i, (i + 2) % 4) for i in range(4)]


def cost(flops, size, exps=0):
    return pl.CostEstimate(flops=flops, bytes_accessed=size, transcendentals=exps)


def node_id(meta):
    return (meta[0] * 4 + meta[1]) * 2 + meta[2]


def ancestor(parents, node, level, target):
    for m in reversed(range(target, level)):
        node = parents[m * NODES + node]
    return node


def relative(meta, node):
    zh = lax.rem(node // 8 + meta[0], 2)
    x = lax.rem(node // 2, 4)
    c = lax.rem(lax.rem(node, 2) + meta[2], 2)
    return c, x, zh


def prepare_kernel(meta, weight, keys, values, cot, *refs):
    pieces, (rows, upper, lower), refs = refs[:4], refs[4:7], refs[7:]
    held, kept, passed, in_sems, out_sems = refs

    def piece(step):
        row = pl.multiple_of((meta[2] * 4 + step) * PIECE, PIECE)
        column = pl.multiple_of((1 - meta[3]) * HALF, HALF)
        return weight.at[pl.ds(row, PIECE), pl.ds(column, HALF)]

    moves = [
        (keys.at[0 : LEVELS - 1, 0], kept.at[0], rows.at[0]),
        (values.at[0 : LEVELS - 1, 0], kept.at[1], rows.at[1]),
        (cot.at[2:4, 0], passed.at[0], upper),
        (cot.at[0:2, 0], passed.at[1], lower),
    ] + [(piece(i), held.at[i], pieces[i]) for i in range(4)]
    reads = [
        pltpu.make_async_copy(source, middle, in_sems.at[i])
        for i, (source, middle, _) in enumerate(moves)
    ]
    writes = [
        pltpu.make_async_copy(middle, target, out_sems.at[i])
        for i, (_, middle, target) in enumerate(moves)
    ]
    for read in reads:
        read.start()
    for read, write in zip(reads, writes):
        read.wait()
        write.start()
    for write in writes:
        write.wait()


def prepare(meta, weight, keys, values, cot):
    return pl.pallas_call(
        prepare_kernel,
        grid_spec=pltpu.PrefetchScalarGridSpec(
            num_scalar_prefetch=1,
            grid=(),
            in_specs=[ANY] * 4,
            out_specs=[ANY] * 7,
            scratch_shapes=[
                pltpu.VMEM((4, PIECE, HALF), jnp.bfloat16),
                pltpu.VMEM((2, LEVELS - 1, SEG, HD), jnp.bfloat16),
                pltpu.VMEM((2, 2, SEG, FEATURES), jnp.bfloat16),
                pltpu.SemaphoreType.DMA((8,)),
                pltpu.SemaphoreType.DMA((8,)),
            ],
        ),
        out_shape=[
            *[jax.ShapeDtypeStruct((PIECE, HALF), jnp.bfloat16)] * 4,
            jax.ShapeDtypeStruct((2, LEVELS - 1, SEG, HD), jnp.bfloat16),
            jax.ShapeDtypeStruct((2, SEG, FEATURES), jnp.bfloat16),
            jax.ShapeDtypeStruct((2, SEG, FEATURES), jnp.bfloat16),
        ],
        compiler_params=PARAMS,
        cost_estimate=cost(0, 12 * 2**20),
        name="prepare",
    )(meta, weight, keys, values, cot)


def tie_kernel(*refs):
    pass


def tie(*arrays):
    return pl.pallas_call(
        tie_kernel,
        in_specs=[ANY] * len(arrays),
        out_specs=[ANY] * len(arrays),
        out_shape=[jax.ShapeDtypeStruct(a.shape, a.dtype) for a in arrays],
        input_output_aliases={i: i for i in range(len(arrays))},
        name="tie",
    )(*arrays)


def early_kernel(meta, own, above, below, w0, w1, w2, out):
    total = sum(
        lax.dot_general(
            cot[...].reshape(2 * SEG, FEATURES), w[...], NT, preferred_element_type=jnp.float32
        )
        for cot, w in ((own, w0), (above, w1), (below, w2))
    )
    out[...] = total.reshape(out.shape)


def late_kernel(meta, across, weight, early, token, *outs):
    total = lax.dot_general(
        across[...].reshape(2 * SEG, FEATURES),
        weight[...],
        NT,
        preferred_element_type=jnp.float32,
    )
    for i in range(2):
        outs[i][...] = early[i] + total[i * SEG : (i + 1) * SEG]


def feature_spec(step):
    def index(n, meta):
        return n, meta[3] * 4 + lax.rem(meta[4] + step, 4)

    return pl.BlockSpec((ROWS, FEATURES), index)


def early_product(meta, own, above, below, weight):
    whole = pl.BlockSpec((2, SEG, FEATURES), lambda n, *_: (0, 0, 0))
    return pl.pallas_call(
        early_kernel,
        grid_spec=pltpu.PrefetchScalarGridSpec(
            num_scalar_prefetch=1,
            grid=(4,),
            in_specs=[whole] * 3 + [feature_spec(step) for step in (0, 1, 3)],
            out_specs=pl.BlockSpec((2, SEG, ROWS), lambda n, *_: (0, 0, n)),
        ),
        out_shape=jax.ShapeDtypeStruct((2, SEG, FEATURES), jnp.float32),
        compiler_params=PARAMS,
        cost_estimate=cost(3 * SEG * 1024 * HALF, 2 * 1024 * HALF),
        name="early_product",
    )(meta, own, above, below, weight, weight, weight)


def late_product(meta, across, weight, early, token):
    whole = pl.BlockSpec((2, SEG, FEATURES), lambda n, *_: (0, 0, 0))
    return pl.pallas_call(
        late_kernel,
        grid_spec=pltpu.PrefetchScalarGridSpec(
            num_scalar_prefetch=1,
            grid=(4,),
            in_specs=[
                whole,
                feature_spec(2),
                pl.BlockSpec((2, SEG, ROWS), lambda n, *_: (0, 0, n)),
                ANY,
            ],
            out_specs=[pl.BlockSpec((SEG, ROWS), lambda n, *_: (0, n))] * 2,
        ),
        out_shape=[jax.ShapeDtypeStruct((SEG, FEATURES), jnp.float32)] * 2,
        compiler_params=PARAMS,
        cost_estimate=cost(SEG * 1024 * HALF, 2 * 1024 * 1024),
        name="late_product",
    )(meta, across, weight, early, token)


def product_kernel(partner, meta, own, above, below, across, *refs):
    count = 8 if partner else 1
    weights, refs = refs[:count], refs[count:]
    outs, (cots, held, cot_sems, sems) = refs[1:3], refs[3:]
    step = pl.program_id(0)

    def place(source, offset, sem, rows):
        column = pl.multiple_of(lax.rem(meta[4] + offset, 4) * FEATURES, FEATURES)
        target = cots.at[rows, pl.ds(column, FEATURES)]
        return pltpu.make_async_copy(source, target, cot_sems.at[sem])

    def block(q):
        if partner:
            return [
                pltpu.make_async_copy(
                    weights[2 * q + i], held.at[q, pl.ds(i * PIECE, PIECE)], sems.at[q, i]
                )
                for i in range(2)
            ]
        column = pl.multiple_of(meta[3] * HALF, HALF)
        source = weights[0].at[q * ROWS : (q + 1) * ROWS, pl.ds(column, HALF)]
        return [pltpu.make_async_copy(source, held.at[q], sems.at[q, 0])]

    upper, lower = pl.ds(0, SEG), pl.ds(SEG, SEG)
    moves = [
        place(part.at[i], offset, 2 * k + i, rows)
        for k, (part, offset) in enumerate(((own, 0), (above, 1), (below, 3), (across, 2)))
        for i, rows in enumerate((upper, lower))
    ]
    blocks = [block(q) for q in range(4)]

    @pl.when(step == 0)
    def _():
        for move in moves + blocks[0]:
            move.start()
        for move in moves + blocks[0]:
            move.wait()
        for move in blocks[1] + blocks[2] + blocks[3]:
            move.start()

    for q in range(1, 4):

        @pl.when(step == q)
        def _(q=q):
            for move in blocks[q]:
                move.wait()

    total = lax.dot_general(cots[...], held[step], NT, preferred_element_type=jnp.float32)
    for i in range(2):
        part = total[i * SEG : (i + 1) * SEG]
        if partner:
            outs[i][0] = part[:, :PIECE].astype(jnp.bfloat16)
            outs[i][1] = part[:, PIECE:].astype(jnp.bfloat16)
        else:
            outs[i][...] = part


def product(partner, meta, cots, weights, token):
    if partner:
        out_shape = [jax.ShapeDtypeStruct((8, SEG, PIECE), jnp.bfloat16)] * 2
        out_specs = [pl.BlockSpec((2, SEG, PIECE), lambda q, *_: (q, 0, 0))] * 2
    else:
        out_shape = [jax.ShapeDtypeStruct((SEG, FEATURES), jnp.float32)] * 2
        out_specs = [pl.BlockSpec((SEG, ROWS), lambda q, *_: (0, q))] * 2
    return pl.pallas_call(
        functools.partial(product_kernel, partner),
        grid_spec=pltpu.PrefetchScalarGridSpec(
            num_scalar_prefetch=1,
            grid=(4,),
            in_specs=[ANY] * (5 + len(weights)),
            out_specs=out_specs,
            scratch_shapes=[
                pltpu.VMEM((2 * SEG, HALF), jnp.bfloat16),
                pltpu.VMEM((4, ROWS, HALF), jnp.bfloat16),
                pltpu.SemaphoreType.DMA((8,)),
                pltpu.SemaphoreType.DMA((4, 2)),
            ],
        ),
        out_shape=out_shape,
        compiler_params=PARAMS,
        cost_estimate=cost(4 * SEG * 1024 * HALF, 2 * 1024 * HALF + 8 * SEG * 1024),
        name="partner_product" if partner else "own_product",
    )(meta, *cots, *weights, token)


def pair_index(level, target):
    return level * (level - 1) // 2 + target


PAIRS = [(level, m) for level in range(LEVELS) for m in range(level)]


def probs_kernel(meta, parents, lengths, query, own_key, mine, other, *refs):
    outs, picked, sems = refs[1:5], refs[5], refs[6]
    me = node_id(meta)

    @pl.when(pl.program_id(0) == 0)
    def _():
        copies = []
        for i, (level, m) in enumerate(PAIRS):
            c, x, zh = relative(meta, ancestor(parents, me, level, m))
            for part in range(2):
                pair = [
                    pltpu.make_async_copy(
                        source.at[x, zh, part, m], picked.at[i, part], sems.at[i, part]
                    )
                    for source in (mine, other)
                ]
                pl.when(c == 0)(pair[0].start)
                pl.when(c == 1)(pair[1].start)
                copies.append(pair[0])
        for copy in copies:
            copy.wait()

    for level in reversed(range(LEVELS)):
        q = jnp.concatenate(
            [query[level, 0, :, i * HD : (i + 1) * HD] for i in range(BATCH)], axis=0
        )
        blocks = []
        for m in range(level + 1):
            key = picked[pair_index(level, m), 0] if m < level else own_key[level, 0]
            s = lax.dot_general(key, q, NT, preferred_element_type=jnp.float32)
            length = lengths[m * NODES + ancestor(parents, me, level, m)]
            position = lax.broadcasted_iota(jnp.int32, s.shape, 0)
            allowed = position < length
            if m == level:
                asked = lax.broadcasted_iota(jnp.int32, s.shape, 1) & (SEG - 1)
                allowed = allowed & (position <= asked)
            blocks.append(jnp.where(allowed, s, MASKED))
        top = functools.reduce(
            jnp.maximum, [jnp.max(s, axis=0, keepdims=True) for s in blocks]
        )
        exps = [jnp.exp2((s - top) * EXP2_SCALE) for s in blocks]
        inverse = 1.0 / sum(jnp.sum(e, axis=0, keepdims=True) for e in exps)
        for m in range(level + 1):
            outs[level][0, m * SEG : (m + 1) * SEG] = (exps[m] * inverse).astype(jnp.bfloat16)


def probs(meta, parents, lengths, queries, key_rows, mine, other, token):
    width = BATCH * HD
    counts = [(level + 1) * SEG for level in range(LEVELS)]
    total = sum(counts)
    return pl.pallas_call(
        probs_kernel,
        grid_spec=pltpu.PrefetchScalarGridSpec(
            num_scalar_prefetch=3,
            grid=(GROUP // BATCH,),
            in_specs=[
                pl.BlockSpec((LEVELS, 1, SEG, width), lambda h, *_: (0, 0, 0, h)),
                pl.BlockSpec((LEVELS, 1, SEG, HD), lambda h, *_: (0, 0, 0, 0)),
                ANY,
                ANY,
                ANY,
            ],
            out_specs=[
                pl.BlockSpec((1, count, BATCH * SEG), lambda h, *_: (h, 0, 0))
                for count in counts
            ]
            + [pl.BlockSpec((len(PAIRS), 2, SEG, HD), lambda h, *_: (0, 0, 0, 0))],
            scratch_shapes=[pltpu.SemaphoreType.DMA((len(PAIRS), 2))],
        ),
        out_shape=[
            jax.ShapeDtypeStruct((GROUP // BATCH, count, BATCH * SEG), jnp.bfloat16)
            for count in counts
        ]
        + [jax.ShapeDtypeStruct((len(PAIRS), 2, SEG, HD), jnp.bfloat16)],
        compiler_params=PARAMS,
        cost_estimate=cost(
            2 * GROUP * total * SEG * HD, 2 * GROUP * total * SEG, GROUP * total * SEG
        ),
        name="probs",
    )(meta, parents, lengths, queries, key_rows, mine, other, token)


def backward_kernel(
    level, meta, parents, lengths, probs_ref, query, own, partner, own_key, own_value, *refs
):
    if level:
        picked, refs = refs[0], refs[1:]
    refs = refs[2:]
    if level:
        query_out, own_out, ancestor_out, flipped, key_total, value_total = refs
    else:
        query_out, own_out, flipped, key_total, value_total = refs
    first = pair_index(level, 0)
    step = pl.program_id(0)
    blocks = [slice(m * SEG, (m + 1) * SEG) for m in range(level + 1)]

    @pl.when(step == 0)
    def _():
        key_total[...] = jnp.zeros_like(key_total)
        value_total[...] = jnp.zeros_like(value_total)
        for m in range(level + 1):
            key = picked[first + m, 0] if m < level else own_key[0, 0]
            flipped[:, blocks[m]] = key.astype(jnp.float32).T.astype(jnp.bfloat16)

    length = lengths[level * NODES + node_id(meta)]
    valid = lax.broadcasted_iota(jnp.int32, (SEG, HD), 0) < length
    heads = []
    for i in range(BATCH):
        head = step * BATCH + i
        piece = lax.rem(step + meta[2], 2) * 4 + i
        total = own[:, i * HD : (i + 1) * HD] + partner[piece].astype(jnp.float32)
        heads.append(jnp.where(valid, total, 0.0).astype(jnp.bfloat16))
    dout = jnp.concatenate(heads, axis=0)
    q = jnp.concatenate([query[0, 0, :, i * HD : (i + 1) * HD] for i in range(BATCH)], axis=0)
    value = jnp.concatenate(
        [picked[first + m, 1] for m in range(level)] + [own_value[0, 0]], axis=0
    )
    narrow = probs_ref[0]
    wide = narrow.astype(jnp.float32)
    grads = lax.dot_general(value, dout, NT, preferred_element_type=jnp.float32)
    delta = jnp.sum(wide * grads, axis=0, keepdims=True)
    scores = (wide * (grads - delta)).astype(jnp.bfloat16)
    key_total[...] += jnp.dot(scores, q, preferred_element_type=jnp.float32)
    value_total[...] += jnp.dot(narrow, dout, preferred_element_type=jnp.float32)
    query_total = jnp.dot(flipped[...], scores, preferred_element_type=jnp.float32) * SCALE
    for i in range(BATCH):
        part = query_total[:, i * SEG : (i + 1) * SEG]
        query_out[0, 0, :, i * HD : (i + 1) * HD] = part.T.astype(jnp.bfloat16)

    @pl.when(step == GROUP // BATCH - 1)
    def _():
        for m in range(level):
            ancestor_out[m, 0] = (key_total[blocks[m]] * SCALE).astype(jnp.bfloat16)
            ancestor_out[m, 1] = value_total[blocks[m]].astype(jnp.bfloat16)
        own_out[0] = key_total[blocks[level]] * SCALE
        own_out[1] = value_total[blocks[level]]


def backward(
    level, meta, parents, lengths, probabilities, queries, own, partner, key_rows, value_rows,
    picked, query_grad, token,
):
    count = (level + 1) * SEG
    width = BATCH * HD
    out_specs = [
        pl.BlockSpec((1, 1, SEG, width), lambda h, *_: (level, 0, 0, h)),
        pl.BlockSpec((2, SEG, HD), lambda h, *_: (0, 0, 0)),
    ]
    out_shape = [
        jax.ShapeDtypeStruct(queries.shape, jnp.bfloat16),
        jax.ShapeDtypeStruct((2, SEG, HD), jnp.float32),
    ]
    if level:
        out_specs.append(pl.BlockSpec((level, 2, SEG, HD), lambda h, *_: (0, 0, 0, 0)))
        out_shape.append(jax.ShapeDtypeStruct((level, 2, SEG, HD), jnp.bfloat16))
    last = level == LEVELS - 1
    return pl.pallas_call(
        functools.partial(backward_kernel, level),
        grid_spec=pltpu.PrefetchScalarGridSpec(
            num_scalar_prefetch=3,
            grid=(GROUP // BATCH,),
            in_specs=[
                pl.BlockSpec((1, count, BATCH * SEG), lambda h, *_: (h, 0, 0)),
                pl.BlockSpec((1, 1, SEG, width), lambda h, *_: (level, 0, 0, h)),
                pl.BlockSpec((SEG, width), lambda h, *_: (0, h)),
                pl.BlockSpec((8, SEG, PIECE), lambda h, *_: (0, 0, 0)),
                pl.BlockSpec((1, 1, SEG, HD), lambda h, *_: (level, 0, 0, 0)),
                pl.BlockSpec((1, 1, SEG, HD), lambda h, *_: (level, 0, 0, 0)),
            ]
            + [pl.BlockSpec((len(PAIRS), 2, SEG, HD), lambda h, *_: (0, 0, 0, 0))] * min(level, 1)
            + [ANY] * 2,
            out_specs=out_specs,
            scratch_shapes=[
                pltpu.VMEM((HD, count), jnp.bfloat16),
                pltpu.VMEM((count, HD), jnp.float32),
                pltpu.VMEM((count, HD), jnp.float32),
            ],
        ),
        out_shape=out_shape,
        input_output_aliases={} if last else {10 if level else 9: 0},
        compiler_params=PARAMS,
        cost_estimate=cost(8 * GROUP * count * SEG * HD, 2 * GROUP * count * SEG),
        name=f"backward_{level}",
    )(
        meta, parents, lengths, probabilities, queries, own, partner, key_rows, value_rows,
        *[picked] * min(level, 1), query_grad, token,
    )


def spread_kernel(target, meta, parents, *refs):
    terms, outs = refs[:-5], refs[-4:]
    me = node_id(meta)
    sibling = me + 1 - 2 * meta[2]
    other = 8 - 16 * meta[0]
    places = []
    for i in range(len(terms)):
        node = (me, sibling, me + other, sibling + other)[i % 4]
        places.append(ancestor(parents, node, target + 1 + i // 4, target))
    for step, out in enumerate(outs):
        x = lax.rem(meta[1] + step, 4)
        wanted = (meta[0] * 4 + x) * 2 + meta[2]
        total = jnp.zeros((2, SEG, HD), jnp.float32)
        for term, place in zip(terms, places):
            total += jnp.where(place == wanted, term[0].astype(jnp.float32), 0.0)
        out[...] = total.astype(jnp.bfloat16)


def spread(target, meta, parents, terms, token):
    return pl.pallas_call(
        functools.partial(spread_kernel, target),
        grid_spec=pltpu.PrefetchScalarGridSpec(
            num_scalar_prefetch=2,
            grid=(1,),
            in_specs=[pl.BlockSpec((1, 2, SEG, HD), lambda n, *_: (target, 0, 0, 0))] * len(terms)
            + [ANY],
            out_specs=[pl.BlockSpec((2, SEG, HD), lambda n, *_: (0, 0, 0))] * 4,
        ),
        out_shape=[jax.ShapeDtypeStruct((2, SEG, HD), jnp.bfloat16)] * 4,
        compiler_params=SMALL,
        cost_estimate=cost(8 * len(terms) * 2 * SEG * HD, 16 * 2 * SEG * HD),
        name=f"spread_{target}",
    )(meta, parents, *terms, token)


def finish_kernel(*refs):
    owns, parts, outs = refs[:LEVELS], refs[LEVELS:-2], refs[-2:]
    for t in range(LEVELS):
        total = owns[t][...]
        for part in parts[4 * t : 4 * t + 4]:
            total += part[...].astype(jnp.float32)
        for i in range(2):
            outs[i][t, 0] = total[i].astype(jnp.bfloat16)


def finish(owns, parts, shape):
    both = pl.BlockSpec((2, SEG, HD), lambda n: (0, 0, 0))
    return pl.pallas_call(
        finish_kernel,
        grid=(1,),
        in_specs=[both] * (LEVELS + len(parts)),
        out_specs=[pl.BlockSpec((LEVELS, 1, SEG, HD), lambda n: (0, 0, 0, 0))] * 2,
        out_shape=[jax.ShapeDtypeStruct(shape, jnp.bfloat16)] * 2,
        compiler_params=SMALL,
        cost_estimate=cost(16 * SEG * HD, 64 * SEG * HD),
        name="finish",
    )(*owns, *parts)


def local(queries, key_rows, value_rows, cotangent, out_weight, parents, seg_len):
    zh, x, c, zl, y = [lax.axis_index(name) for name in ("zh", "x", "c", "zl", "y")]
    meta = jnp.stack([zh, x, c, zl, y]).astype(jnp.int32)
    parents = parents.reshape(-1)
    lengths = seg_len.reshape(-1)
    *pieces, rows, upper, lower = prepare(meta, out_weight, key_rows, value_rows, cotangent)

    def hop(piece, i):
        if i % 2:
            return lax.ppermute(piece, ("zh", "zl"), ALT)
        return lax.ppermute(piece, "zl", SWAP)

    away = lax.ppermute(rows, "zh", SWAP)
    above = lax.ppermute(upper, "y", DOWN)
    below = lax.ppermute(upper, "y", UP)
    w0, w1 = hop(pieces[0], 0), hop(pieces[1], 1)
    rows, away, above, below, w0, w1, lower, p2, p3 = tie(
        rows, away, above, below, w0, w1, lower, pieces[2], pieces[3]
    )
    mine = lax.all_gather(jnp.stack([rows, away]), "x")
    across = lax.ppermute(below, "y", UP)
    above_low = lax.ppermute(lower, "y", DOWN)
    w2, w3 = hop(p2, 2), hop(p3, 3)
    o0, o1 = lax.ppermute(w0, "c", SWAP), lax.ppermute(w1, "c", SWAP)
    early = early_product(meta, upper, above, below, out_weight)
    across, above_low, w0, w1, w2, w3, o0, o1, lower, mine, early = tie(
        across, above_low, w0, w1, w2, w3, o0, o1, lower, mine, early
    )
    below_low = lax.ppermute(lower, "y", UP)
    across_low = lax.ppermute(above_low, "y", DOWN)
    o2, o3 = lax.ppermute(w2, "c", SWAP), lax.ppermute(w3, "c", SWAP)
    weights = [w0, w1, w2, w3, o0, o1, o2, o3]
    cots = [(lower, above_low, below_low, across_low), (upper, above, below, across)]
    other = lax.ppermute(mine, "c", SWAP)
    table = (meta, parents, lengths)
    owns = [None] * LEVELS
    partners = [None] * LEVELS

    def own_pair(i, token):
        owns[2 * i], owns[2 * i + 1] = product(False, meta, cots[i], [out_weight], token)
        return owns[2 * i]

    def partner_pair(i, token):
        parts = product(True, meta, cots[i], weights, token)
        for j in (1, 0):
            partners[2 * i + j] = lax.ppermute(parts[j], "zl", SWAP)
        return parts[0]

    owns[2], owns[3] = late_product(meta, across, out_weight, early, meta)
    token = partner_pair(1, owns[2])
    *probabilities, picked = probs(*table, queries, key_rows, mine, other, token)
    token = partner_pair(0, picked)
    query_grad = own_pair(0, token)
    own_grads = [None] * LEVELS
    terms = []
    parts = []
    token = query_grad
    for level in (3, 2, 1, 0):
        query_grad, own_grads[level], *rest = backward(
            level, *table, probabilities[level], queries, owns[level], partners[level],
            key_rows, value_rows, picked, query_grad, token,
        )
        if level < 3:
            here, up, across, down = spread(level, meta, parents, terms, query_grad)
            token = here
            parts = [
                here,
                lax.ppermute(up, "x", UP),
                lax.ppermute(down, "x", DOWN),
                lax.ppermute(across, "x", ACROSS),
            ] + parts
        if level:
            near = rest[0]
            sibling = lax.ppermute(near, "c", SWAP)
            terms = [
                near,
                sibling,
                lax.ppermute(near, "zh", SWAP),
                lax.ppermute(sibling, "zh", SWAP),
            ] + terms
    key_grad, value_grad = finish(own_grads, parts, key_rows.shape)
    return (query_grad, key_grad, value_grad)


def solution(mesh):
    fine = Mesh(mesh.devices.reshape(2, 4, 2, 2, 4), ("zh", "x", "c", "zl", "y"))
    rows = P(None, AXES, None, ("zl", "y"))
    in_specs = (rows, rows, rows, rows, P(("zl", "y"), None), P(), P())
    return jax.shard_map(
        local, mesh=fine, in_specs=in_specs, out_specs=(rows, rows, rows), check_vma=False
    )
```

```python
import functools

import jax
import jax.numpy as jnp
from jax import lax
from jax.experimental import pallas as pl
from jax.experimental.pallas import tpu as pltpu
from jax.sharding import Mesh, PartitionSpec as P

HD = 128
SEG = 256
GROUP = 8
BATCH = 4
LEVELS = 4
NODES = 16
FEATURES = 1024
HALF = 4096
PIECE = 128
ROWS = 256
SCALE = 1.0 / HD**0.5
EXP2_SCALE = SCALE * 1.4426950408889634
MASKED = -1e30
NT = (((1,), (1,)), ((), ()))
PARAMS = pltpu.CompilerParams(vmem_limit_bytes=56 * 2**20)
SMALL = pltpu.CompilerParams(vmem_limit_bytes=16 * 2**20)
ANY = pl.BlockSpec(memory_space=pltpu.HBM)
AXES = ("zh", "x", "c")
ALT = [(0, 3), (1, 2), (2, 1), (3, 0)]
SWAP = [(0, 1), (1, 0)]
UP = [(i, (i + 1) % 4) for i in range(4)]
DOWN = [(i, (i + 3) % 4) for i in range(4)]
ACROSS = [(i, (i + 2) % 4) for i in range(4)]


def cost(flops, size, exps=0):
    return pl.CostEstimate(flops=1, bytes_accessed=1, transcendentals=0)


def node_id(meta):
    return (meta[0] * 4 + meta[1]) * 2 + meta[2]


def ancestor(parents, node, level, target):
    for m in reversed(range(target, level)):
        node = parents[m * NODES + node]
    return node


def relative(meta, node):
    zh = lax.rem(node // 8 + meta[0], 2)
    x = lax.rem(node // 2, 4)
    c = lax.rem(lax.rem(node, 2) + meta[2], 2)
    return c, x, zh


def prepare_kernel(meta, weight, cot, *refs):
    pieces, (upper, lower), refs = refs[:4], refs[4:6], refs[6:]
    held, passed, in_sems, out_sems = refs

    def piece(step):
        row = pl.multiple_of((meta[2] * 4 + step) * PIECE, PIECE)
        column = pl.multiple_of((1 - meta[3]) * HALF, HALF)
        return weight.at[pl.ds(row, PIECE), pl.ds(column, HALF)]

    moves = [
        (cot.at[2:4, 0], passed.at[0], upper),
        (cot.at[0:2, 0], passed.at[1], lower),
    ] + [(piece(i), held.at[i], pieces[i]) for i in range(4)]
    reads = [
        pltpu.make_async_copy(source, middle, in_sems.at[i])
        for i, (source, middle, _) in enumerate(moves)
    ]
    writes = [
        pltpu.make_async_copy(middle, target, out_sems.at[i])
        for i, (_, middle, target) in enumerate(moves)
    ]
    for read in reads:
        read.start()
    for read, write in zip(reads, writes):
        read.wait()
        write.start()
    for write in writes:
        write.wait()


def prepare(meta, weight, cot):
    return pl.pallas_call(
        prepare_kernel,
        grid_spec=pltpu.PrefetchScalarGridSpec(
            num_scalar_prefetch=1,
            grid=(),
            in_specs=[ANY] * 2,
            out_specs=[ANY] * 6,
            scratch_shapes=[
                pltpu.VMEM((4, PIECE, HALF), jnp.bfloat16),
                pltpu.VMEM((2, 2, SEG, FEATURES), jnp.bfloat16),
                pltpu.SemaphoreType.DMA((6,)),
                pltpu.SemaphoreType.DMA((6,)),
            ],
        ),
        out_shape=[
            *[jax.ShapeDtypeStruct((PIECE, HALF), jnp.bfloat16)] * 4,
            jax.ShapeDtypeStruct((2, SEG, FEATURES), jnp.bfloat16),
            jax.ShapeDtypeStruct((2, SEG, FEATURES), jnp.bfloat16),
        ],
        compiler_params=PARAMS,
        cost_estimate=cost(0, 12 * 2**20),
        name="prepare",
    )(meta, weight, cot)


def tie_kernel(*refs):
    pass


def tie(*arrays):
    return pl.pallas_call(
        tie_kernel,
        in_specs=[ANY] * len(arrays),
        out_specs=[ANY] * len(arrays),
        out_shape=[jax.ShapeDtypeStruct(a.shape, a.dtype) for a in arrays],
        input_output_aliases={i: i for i in range(len(arrays))},
        name="tie",
    )(*arrays)


def blocks_kernel(count, added, meta, *refs):
    cots, weights, refs = refs[:count], refs[count : 2 * count], refs[2 * count :]
    total = sum(
        lax.dot_general(
            cot[...].reshape(2 * SEG, FEATURES), weight[...], NT, preferred_element_type=jnp.float32
        )
        for cot, weight in zip(cots, weights)
    ).reshape(2, SEG, ROWS)
    if added:
        total += refs[0][...]
    refs[-1][...] = total


def feature_spec(step):
    def index(n, meta):
        return n, meta[3] * 4 + lax.rem(meta[4] + step, 4)

    return pl.BlockSpec((ROWS, FEATURES), index)


def blocks_product(meta, cots, steps, weight, earlier, token):
    count = len(cots)
    whole = pl.BlockSpec((2, SEG, FEATURES), lambda n, *_: (0, 0, 0))
    part = pl.BlockSpec((2, SEG, ROWS), lambda n, *_: (0, 0, n))
    return pl.pallas_call(
        functools.partial(blocks_kernel, count, len(earlier)),
        grid_spec=pltpu.PrefetchScalarGridSpec(
            num_scalar_prefetch=1,
            grid=(4,),
            in_specs=[whole] * count
            + [feature_spec(step) for step in steps]
            + [part] * len(earlier)
            + [ANY],
            out_specs=part,
        ),
        out_shape=jax.ShapeDtypeStruct((2, SEG, FEATURES), jnp.float32),
        compiler_params=PARAMS,
        cost_estimate=cost(count * SEG * 1024 * HALF, 2 * 1024 * HALF),
        name="own_product",
    )(meta, *cots, *[weight] * count, *earlier, token)


def product_kernel(meta, own, above, below, across, *refs):
    weights, refs = refs[:8], refs[8:]
    outs, (cots, held, cot_sems, sems) = refs[1:3], refs[3:]
    step = pl.program_id(0)

    def place(source, offset, sem, rows):
        column = pl.multiple_of(lax.rem(meta[4] + offset, 4) * FEATURES, FEATURES)
        target = cots.at[rows, pl.ds(column, FEATURES)]
        return pltpu.make_async_copy(source, target, cot_sems.at[sem])

    def block(q):
        return [
            pltpu.make_async_copy(
                weights[2 * q + i], held.at[q, pl.ds(i * PIECE, PIECE)], sems.at[q, i]
            )
            for i in range(2)
        ]

    upper, lower = pl.ds(0, SEG), pl.ds(SEG, SEG)
    moves = [
        place(part.at[i], offset, 2 * k + i, rows)
        for k, (part, offset) in enumerate(((own, 0), (above, 1), (below, 3), (across, 2)))
        for i, rows in enumerate((upper, lower))
    ]
    blocks = [block(q) for q in range(4)]

    @pl.when(step == 0)
    def _():
        for move in moves + blocks[0]:
            move.start()
        for move in moves + blocks[0]:
            move.wait()
        for move in blocks[1] + blocks[2] + blocks[3]:
            move.start()

    for q in range(1, 4):

        @pl.when(step == q)
        def _(q=q):
            for move in blocks[q]:
                move.wait()

    total = lax.dot_general(cots[...], held[step], NT, preferred_element_type=jnp.float32)
    for i in range(2):
        part = total[i * SEG : (i + 1) * SEG]
        outs[i][0] = part[:, :PIECE].astype(jnp.bfloat16)
        outs[i][1] = part[:, PIECE:].astype(jnp.bfloat16)


def product(meta, cots, weights, token):
    out_shape = [jax.ShapeDtypeStruct((8, SEG, PIECE), jnp.bfloat16)] * 2
    out_specs = [pl.BlockSpec((2, SEG, PIECE), lambda q, *_: (q, 0, 0))] * 2
    return pl.pallas_call(
        product_kernel,
        grid_spec=pltpu.PrefetchScalarGridSpec(
            num_scalar_prefetch=1,
            grid=(4,),
            in_specs=[ANY] * (5 + len(weights)),
            out_specs=out_specs,
            scratch_shapes=[
                pltpu.VMEM((2 * SEG, HALF), jnp.bfloat16),
                pltpu.VMEM((4, ROWS, HALF), jnp.bfloat16),
                pltpu.SemaphoreType.DMA((8,)),
                pltpu.SemaphoreType.DMA((4, 2)),
            ],
        ),
        out_shape=out_shape,
        compiler_params=PARAMS,
        cost_estimate=cost(4 * SEG * 1024 * HALF, 2 * 1024 * HALF + 8 * SEG * 1024),
        name="partner_product",
    )(meta, *cots, *weights, token)


def pair_index(level, target):
    return level * (level - 1) // 2 + target


PAIRS = [(level, m) for level in range(LEVELS) for m in range(level)]


def pick_kernel(meta, parents, mine, *refs):
    outs, sems = refs[:2], refs[2]
    copies = []
    for i, (level, m) in enumerate(PAIRS):
        for side in range(2):
            me = node_id(meta)
            if side:
                me = me + 1 - 2 * meta[2]
            c, x, zh = relative(meta, ancestor(parents, me, level, m))
            for part in range(2):
                copy = pltpu.make_async_copy(
                    mine.at[x, zh, part, m], outs[side].at[i, part], sems.at[side, i, part]
                )
                copies.append((c == 0, copy))
    for held, copy in copies:
        pl.when(held)(copy.start)
    for held, copy in copies:
        pl.when(held)(copy.wait)


def pick(meta, parents, mine):
    shape = (len(PAIRS), 2, SEG, HD)
    return pl.pallas_call(
        pick_kernel,
        grid_spec=pltpu.PrefetchScalarGridSpec(
            num_scalar_prefetch=2,
            grid=(1,),
            in_specs=[ANY],
            out_specs=[pl.BlockSpec(shape, lambda *_: (0, 0, 0, 0))] * 2,
            scratch_shapes=[pltpu.SemaphoreType.DMA((2, len(PAIRS), 2))],
        ),
        out_shape=[jax.ShapeDtypeStruct(shape, jnp.bfloat16)] * 2,
        compiler_params=PARAMS,
        cost_estimate=cost(0, 0),
        name="pick",
    )(meta, parents, mine)


def probs_kernel(meta, parents, lengths, query, own_key, mine, other, *refs):
    outs, picked, sems = refs[1:5], refs[5], refs[6]
    me = node_id(meta)

    @pl.when(pl.program_id(0) == 0)
    def _():
        copies = []
        for i, (level, m) in enumerate(PAIRS):
            c = relative(meta, ancestor(parents, me, level, m))[0]
            for part in range(2):
                pair = [
                    pltpu.make_async_copy(
                        source.at[i, part], picked.at[i, part], sems.at[i, part]
                    )
                    for source in (mine, other)
                ]
                pl.when(c == 0)(pair[0].start)
                pl.when(c == 1)(pair[1].start)
                copies.append(pair[0])
        for copy in copies:
            copy.wait()

    for level in reversed(range(LEVELS)):
        q = jnp.concatenate(
            [query[level, 0, :, i * HD : (i + 1) * HD] for i in range(BATCH)], axis=0
        )
        blocks = []
        for m in range(level + 1):
            key = picked[pair_index(level, m), 0] if m < level else own_key[level, 0]
            s = lax.dot_general(key, q, NT, preferred_element_type=jnp.float32)
            length = lengths[m * NODES + ancestor(parents, me, level, m)]
            position = lax.broadcasted_iota(jnp.int32, s.shape, 0)
            allowed = position < length
            if m == level:
                asked = lax.broadcasted_iota(jnp.int32, s.shape, 1) & (SEG - 1)
                allowed = allowed & (position <= asked)
            blocks.append(jnp.where(allowed, s, MASKED))
        top = functools.reduce(
            jnp.maximum, [jnp.max(s, axis=0, keepdims=True) for s in blocks]
        )
        exps = [jnp.exp2((s - top) * EXP2_SCALE) for s in blocks]
        inverse = 1.0 / sum(jnp.sum(e, axis=0, keepdims=True) for e in exps)
        for m in range(level + 1):
            outs[level][0, m * SEG : (m + 1) * SEG] = (exps[m] * inverse).astype(jnp.bfloat16)


def probs(meta, parents, lengths, queries, key_rows, mine, other, token):
    width = BATCH * HD
    counts = [(level + 1) * SEG for level in range(LEVELS)]
    total = sum(counts)
    return pl.pallas_call(
        probs_kernel,
        grid_spec=pltpu.PrefetchScalarGridSpec(
            num_scalar_prefetch=3,
            grid=(GROUP // BATCH,),
            in_specs=[
                pl.BlockSpec((LEVELS, 1, SEG, width), lambda h, *_: (0, 0, 0, h)),
                pl.BlockSpec((LEVELS, 1, SEG, HD), lambda h, *_: (0, 0, 0, 0)),
                ANY,
                ANY,
                ANY,
            ],
            out_specs=[
                pl.BlockSpec((1, count, BATCH * SEG), lambda h, *_: (h, 0, 0))
                for count in counts
            ]
            + [pl.BlockSpec((len(PAIRS), 2, SEG, HD), lambda h, *_: (0, 0, 0, 0))],
            scratch_shapes=[pltpu.SemaphoreType.DMA((len(PAIRS), 2))],
        ),
        out_shape=[
            jax.ShapeDtypeStruct((GROUP // BATCH, count, BATCH * SEG), jnp.bfloat16)
            for count in counts
        ]
        + [jax.ShapeDtypeStruct((len(PAIRS), 2, SEG, HD), jnp.bfloat16)],
        compiler_params=PARAMS,
        cost_estimate=cost(
            2 * GROUP * total * SEG * HD, 2 * GROUP * total * SEG, GROUP * total * SEG
        ),
        name="probs",
    )(meta, parents, lengths, queries, key_rows, mine, other, token)


def backward_kernel(
    level, meta, parents, lengths, probs_ref, query, own, partner, own_key, own_value, *refs
):
    if level:
        picked, refs = refs[0], refs[1:]
    refs = refs[2:]
    if level:
        query_out, own_out, ancestor_out, flipped, key_total, value_total = refs
    else:
        query_out, own_out, flipped, key_total, value_total = refs
    first = pair_index(level, 0)
    step = pl.program_id(0)
    blocks = [slice(m * SEG, (m + 1) * SEG) for m in range(level + 1)]

    @pl.when(step == 0)
    def _():
        key_total[...] = jnp.zeros_like(key_total)
        value_total[...] = jnp.zeros_like(value_total)
        for m in range(level + 1):
            key = picked[first + m, 0] if m < level else own_key[0, 0]
            flipped[:, blocks[m]] = key.astype(jnp.float32).T.astype(jnp.bfloat16)

    length = lengths[level * NODES + node_id(meta)]
    valid = lax.broadcasted_iota(jnp.int32, (SEG, HD), 0) < length
    heads = []
    for i in range(BATCH):
        head = step * BATCH + i
        piece = lax.rem(step + meta[2], 2) * 4 + i
        total = own[0, :, i * HD : (i + 1) * HD] + partner[piece].astype(jnp.float32)
        heads.append(jnp.where(valid, total, 0.0).astype(jnp.bfloat16))
    dout = jnp.concatenate(heads, axis=0)
    q = jnp.concatenate([query[0, 0, :, i * HD : (i + 1) * HD] for i in range(BATCH)], axis=0)
    value = jnp.concatenate(
        [picked[first + m, 1] for m in range(level)] + [own_value[0, 0]], axis=0
    )
    narrow = probs_ref[0]
    wide = narrow.astype(jnp.float32)
    grads = lax.dot_general(value, dout, NT, preferred_element_type=jnp.float32)
    delta = jnp.sum(wide * grads, axis=0, keepdims=True)
    scores = (wide * (grads - delta)).astype(jnp.bfloat16)
    key_total[...] += jnp.dot(scores, q, preferred_element_type=jnp.float32)
    value_total[...] += jnp.dot(narrow, dout, preferred_element_type=jnp.float32)
    query_total = jnp.dot(flipped[...], scores, preferred_element_type=jnp.float32) * SCALE
    for i in range(BATCH):
        part = query_total[:, i * SEG : (i + 1) * SEG]
        query_out[0, 0, :, i * HD : (i + 1) * HD] = part.T.astype(jnp.bfloat16)

    @pl.when(step == GROUP // BATCH - 1)
    def _():
        for m in range(level):
            ancestor_out[m, 0] = (key_total[blocks[m]] * SCALE).astype(jnp.bfloat16)
            ancestor_out[m, 1] = value_total[blocks[m]].astype(jnp.bfloat16)
        own_out[0] = key_total[blocks[level]] * SCALE
        own_out[1] = value_total[blocks[level]]


def backward(
    level, meta, parents, lengths, probabilities, queries, own, partner, key_rows, value_rows,
    picked, query_grad, token,
):
    count = (level + 1) * SEG
    width = BATCH * HD
    out_specs = [
        pl.BlockSpec((1, 1, SEG, width), lambda h, *_: (level, 0, 0, h)),
        pl.BlockSpec((2, SEG, HD), lambda h, *_: (0, 0, 0)),
    ]
    out_shape = [
        jax.ShapeDtypeStruct(queries.shape, jnp.bfloat16),
        jax.ShapeDtypeStruct((2, SEG, HD), jnp.float32),
    ]
    if level:
        out_specs.append(pl.BlockSpec((level, 2, SEG, HD), lambda h, *_: (0, 0, 0, 0)))
        out_shape.append(jax.ShapeDtypeStruct((level, 2, SEG, HD), jnp.bfloat16))
    last = level == LEVELS - 1
    return pl.pallas_call(
        functools.partial(backward_kernel, level),
        grid_spec=pltpu.PrefetchScalarGridSpec(
            num_scalar_prefetch=3,
            grid=(GROUP // BATCH,),
            in_specs=[
                pl.BlockSpec((1, count, BATCH * SEG), lambda h, *_: (h, 0, 0)),
                pl.BlockSpec((1, 1, SEG, width), lambda h, *_: (level, 0, 0, h)),
                pl.BlockSpec((1, SEG, width), lambda h, *_: (level % 2, 0, h)),
                pl.BlockSpec((8, SEG, PIECE), lambda h, *_: (0, 0, 0)),
                pl.BlockSpec((1, 1, SEG, HD), lambda h, *_: (level, 0, 0, 0)),
                pl.BlockSpec((1, 1, SEG, HD), lambda h, *_: (level, 0, 0, 0)),
            ]
            + [pl.BlockSpec((len(PAIRS), 2, SEG, HD), lambda h, *_: (0, 0, 0, 0))] * min(level, 1)
            + [ANY] * 2,
            out_specs=out_specs,
            scratch_shapes=[
                pltpu.VMEM((HD, count), jnp.bfloat16),
                pltpu.VMEM((count, HD), jnp.float32),
                pltpu.VMEM((count, HD), jnp.float32),
            ],
        ),
        out_shape=out_shape,
        input_output_aliases={} if last else {10 if level else 9: 0},
        compiler_params=PARAMS,
        cost_estimate=cost(8 * GROUP * count * SEG * HD, 2 * GROUP * count * SEG),
        name=f"backward_{level}",
    )(
        meta, parents, lengths, probabilities, queries, own, partner, key_rows, value_rows,
        *[picked] * min(level, 1), query_grad, token,
    )


def spread_kernel(target, meta, parents, *refs):
    terms, outs = refs[:-5], refs[-4:]
    me = node_id(meta)
    sibling = me + 1 - 2 * meta[2]
    places = []
    for i in range(len(terms)):
        node = sibling if i % 2 else me
        places.append(ancestor(parents, node, target + 1 + i // 2, target))
    for step, out in enumerate(outs):
        x = lax.rem(meta[1] + step, 4)
        for zh in range(2):
            wanted = (zh * 4 + x) * 2 + meta[2]
            total = jnp.zeros((2, SEG, HD), jnp.float32)
            for term, place in zip(terms, places):
                total += jnp.where(place == wanted, term[0].astype(jnp.float32), 0.0)
            out[zh] = total.astype(jnp.bfloat16)


def spread(target, meta, parents, terms, token):
    whole = pl.BlockSpec((2, 2, SEG, HD), lambda n, *_: (0, 0, 0, 0))
    return pl.pallas_call(
        functools.partial(spread_kernel, target),
        grid_spec=pltpu.PrefetchScalarGridSpec(
            num_scalar_prefetch=2,
            grid=(1,),
            in_specs=[pl.BlockSpec((1, 2, SEG, HD), lambda n, *_: (target, 0, 0, 0))] * len(terms)
            + [ANY],
            out_specs=[whole] * 4,
        ),
        out_shape=[jax.ShapeDtypeStruct((2, 2, SEG, HD), jnp.bfloat16)] * 4,
        compiler_params=SMALL,
        cost_estimate=cost(0, 0),
        name=f"spread_{target}",
    )(meta, parents, *terms, token)


def collect_kernel(meta, *refs):
    parts, (kept, given) = refs[:4], refs[5:]
    kept[...] = sum(part[meta[0]].astype(jnp.float32) for part in parts)
    given[...] = sum(part[1 - meta[0]].astype(jnp.float32) for part in parts).astype(jnp.bfloat16)


def collect(meta, parts, token):
    whole = pl.BlockSpec((2, 2, SEG, HD), lambda n, *_: (0, 0, 0, 0))
    half = pl.BlockSpec((2, SEG, HD), lambda n, *_: (0, 0, 0))
    return pl.pallas_call(
        collect_kernel,
        grid_spec=pltpu.PrefetchScalarGridSpec(
            num_scalar_prefetch=1,
            grid=(1,),
            in_specs=[whole] * 4 + [ANY],
            out_specs=[half] * 2,
        ),
        out_shape=[
            jax.ShapeDtypeStruct((2, SEG, HD), jnp.float32),
            jax.ShapeDtypeStruct((2, SEG, HD), jnp.bfloat16),
        ],
        compiler_params=SMALL,
        cost_estimate=cost(0, 0),
        name="collect",
    )(meta, *parts, token)


def finish_kernel(*refs):
    owns, parts, outs = refs[:LEVELS], refs[LEVELS:-2], refs[-2:]
    for t in range(LEVELS):
        total = owns[t][...]
        for part in parts[2 * t : 2 * t + 2]:
            total += part[...].astype(jnp.float32)
        for i in range(2):
            outs[i][t, 0] = total[i].astype(jnp.bfloat16)


def finish(owns, parts, shape):
    both = pl.BlockSpec((2, SEG, HD), lambda n: (0, 0, 0))
    return pl.pallas_call(
        finish_kernel,
        grid=(1,),
        in_specs=[both] * (LEVELS + len(parts)),
        out_specs=[pl.BlockSpec((LEVELS, 1, SEG, HD), lambda n: (0, 0, 0, 0))] * 2,
        out_shape=[jax.ShapeDtypeStruct(shape, jnp.bfloat16)] * 2,
        compiler_params=SMALL,
        cost_estimate=cost(16 * SEG * HD, 64 * SEG * HD),
        name="finish",
    )(*owns, *parts)


def local(queries, key_rows, value_rows, cotangent, out_weight, parents, seg_len):
    zh, x, c, zl, y = [lax.axis_index(name) for name in ("zh", "x", "c", "zl", "y")]
    meta = jnp.stack([zh, x, c, zl, y]).astype(jnp.int32)
    parents = parents.reshape(-1)
    lengths = seg_len.reshape(-1)
    table = (meta, parents, lengths)
    rows = jnp.stack([key_rows[: LEVELS - 1, 0], value_rows[: LEVELS - 1, 0]])
    away = lax.ppermute(rows, "zh", SWAP)
    *pieces, upper, lower = prepare(meta, out_weight, cotangent)
    rows, away, upper, *pieces = tie(rows, away, upper, *pieces)
    mine = lax.all_gather(jnp.stack([rows, away]), "x")

    def hop(piece, i):
        if i % 2:
            return lax.ppermute(piece, ("zh", "zl"), ALT)
        return lax.ppermute(piece, "zl", SWAP)

    above = lax.ppermute(upper, "y", DOWN)
    below = lax.ppermute(upper, "y", UP)
    w0, w1 = hop(pieces[0], 0), hop(pieces[1], 1)
    above, below, w0, w1, lower, p2, p3 = tie(
        above, below, w0, w1, lower, pieces[2], pieces[3]
    )
    across = lax.ppermute(below, "y", UP)
    above_low = lax.ppermute(lower, "y", DOWN)
    w2, w3 = hop(p2, 2), hop(p3, 3)
    early = blocks_product(meta, [upper, above, below], (0, 1, 3), out_weight, [], meta)
    mine, early = tie(mine, early)
    mine, other = pick(meta, parents, mine)
    other = lax.ppermute(other, "c", SWAP)
    *probabilities, picked = probs(*table, queries, key_rows, mine, other, early)
    across, above_low, w0, w1, w2, w3, lower, early, picked = tie(
        across, above_low, w0, w1, w2, w3, lower, early, picked
    )
    below_low = lax.ppermute(lower, "y", UP)
    across_low = lax.ppermute(above_low, "y", DOWN)
    weights = [w0, w1, w2, w3]
    weights += [lax.ppermute(piece, "c", SWAP) for piece in weights]
    partners = [None] * LEVELS

    def partner_pair(i, cots, token):
        parts = product(meta, cots, weights, token)
        for j in (1, 0):
            partners[2 * i + j] = lax.ppermute(parts[j], "zl", SWAP)
        return parts[0]

    own_high = blocks_product(meta, [across], (2,), out_weight, [early], meta)
    token = partner_pair(1, (upper, above, below, across), own_high)
    early_low = blocks_product(meta, [lower, above_low], (0, 1), out_weight, [], token)
    token = partner_pair(0, (lower, above_low, below_low, across_low), early_low)
    own_grads = [None] * LEVELS
    terms = [None] * 6
    moved = [None] * (LEVELS - 1)
    parts = [None] * 6

    def back(level, own, query_grad, token):
        query_grad, own_grads[level], *rest = backward(
            level, *table, probabilities[level], queries, own, partners[level],
            key_rows, value_rows, picked, query_grad, token,
        )
        if level:
            terms[2 * level - 2] = rest[0]
            terms[2 * level - 1] = lax.ppermute(rest[0], "c", SWAP)
        return query_grad

    def spread_out(target, token):
        here, up, across, down = spread(target, meta, parents, terms[2 * target :], token)
        moved[target] = [
            here,
            lax.ppermute(up, "x", UP),
            lax.ppermute(down, "x", DOWN),
            lax.ppermute(across, "x", ACROSS),
        ]
        return here

    def bring(target, token):
        kept, given = collect(meta, moved[target], token)
        parts[2 * target] = kept
        parts[2 * target + 1] = lax.ppermute(given, "zh", SWAP)
        return kept

    query_grad = back(3, own_high, token, token)
    own_low = blocks_product(
        meta, [below_low, across_low], (3, 2), out_weight, [early_low], query_grad
    )
    token = spread_out(2, own_low)
    query_grad = back(2, own_high, query_grad, token)
    token = spread_out(1, query_grad)
    query_grad = back(1, own_low, query_grad, token)
    token = bring(2, query_grad)
    token = spread_out(0, token)
    query_grad = back(0, own_low, query_grad, token)
    token = bring(1, query_grad)
    bring(0, token)
    key_grad, value_grad = finish(own_grads, parts, key_rows.shape)
    return (query_grad, key_grad, value_grad)


def solution(mesh):
    fine = Mesh(mesh.devices.reshape(2, 4, 2, 2, 4), ("zh", "x", "c", "zl", "y"))
    rows = P(None, AXES, None, ("zl", "y"))
    in_specs = (rows, rows, rows, rows, P(("zl", "y"), None), P(), P())
    return jax.shard_map(
        local, mesh=fine, in_specs=in_specs, out_specs=(rows, rows, rows), check_vma=False
    )
```

```python
import functools

import jax
import jax.numpy as jnp
from jax import lax
from jax.experimental import pallas as pl
from jax.experimental.pallas import tpu as pltpu
from jax.sharding import Mesh, PartitionSpec as P

HD = 128
SEG = 256
GROUP = 8
BATCH = 4
LEVELS = 4
NODES = 16
FEATURES = 1024
HALF = 4096
PIECE = 128
ROWS = 256
SCALE = 1.0 / HD**0.5
EXP2_SCALE = SCALE * 1.4426950408889634
MASKED = -1e30
NT = (((1,), (1,)), ((), ()))
PARAMS = pltpu.CompilerParams(vmem_limit_bytes=56 * 2**20)
SMALL = pltpu.CompilerParams(vmem_limit_bytes=16 * 2**20)
LIGHT = pltpu.CompilerParams(vmem_limit_bytes=24 * 2**20)
LARGE = pltpu.CompilerParams(vmem_limit_bytes=48 * 2**20)
MIDDLE = pltpu.CompilerParams(vmem_limit_bytes=32 * 2**20)
ANY = pl.BlockSpec(memory_space=pltpu.HBM)
FREE = pl.BlockSpec(memory_space=pl.ANY)
AXES = ("zh", "x", "c")
ALT = [(0, 3), (1, 2), (2, 1), (3, 0)]
SWAP = [(0, 1), (1, 0)]
UP = [(i, (i + 1) % 4) for i in range(4)]
DOWN = [(i, (i + 3) % 4) for i in range(4)]
ACROSS = [(i, (i + 2) % 4) for i in range(4)]


TOKEN = pl.BlockSpec((8, HD), lambda *_: (0, 0))
TOKEN_SHAPE = jax.ShapeDtypeStruct((8, HD), jnp.float32)


def cost(flops, size, exps=0):
    return pl.CostEstimate(flops=1, bytes_accessed=1, transcendentals=0)


def node_id(meta):
    return (meta[0] * 4 + meta[1]) * 2 + meta[2]


def ancestor(parents, node, level, target):
    for m in reversed(range(target, level)):
        node = parents[m * NODES + node]
    return node


def relative(meta, node):
    zh = lax.rem(node // 8 + meta[0], 2)
    x = lax.rem(node // 2, 4)
    c = lax.rem(lax.rem(node, 2) + meta[2], 2)
    return c, x, zh


def prepare_kernel(meta, weight, cot, *refs):
    pieces, (upper, lower), refs = refs[:4], refs[4:6], refs[6:]
    held, passed, in_sems, out_sems = refs

    def piece(step):
        row = pl.multiple_of((meta[2] * 4 + step) * PIECE, PIECE)
        column = pl.multiple_of((1 - meta[3]) * HALF, HALF)
        return weight.at[pl.ds(row, PIECE), pl.ds(column, HALF)]

    moves = [
        (cot.at[2:4, 0], passed.at[0], upper),
        (cot.at[0:2, 0], passed.at[1], lower),
    ] + [(piece(i), held.at[i], pieces[i]) for i in range(4)]
    reads = [
        pltpu.make_async_copy(source, middle, in_sems.at[i])
        for i, (source, middle, _) in enumerate(moves)
    ]
    writes = [
        pltpu.make_async_copy(middle, target, out_sems.at[i])
        for i, (_, middle, target) in enumerate(moves)
    ]
    for read in reads:
        read.start()
    for read, write in zip(reads, writes):
        read.wait()
        write.start()
    for write in writes:
        write.wait()


def prepare(meta, weight, cot):
    return pl.pallas_call(
        prepare_kernel,
        grid_spec=pltpu.PrefetchScalarGridSpec(
            num_scalar_prefetch=1,
            grid=(),
            in_specs=[ANY] * 2,
            out_specs=[ANY] * 6,
            scratch_shapes=[
                pltpu.VMEM((4, PIECE, HALF), jnp.bfloat16),
                pltpu.VMEM((2, 2, SEG, FEATURES), jnp.bfloat16),
                pltpu.SemaphoreType.DMA((6,)),
                pltpu.SemaphoreType.DMA((6,)),
            ],
        ),
        out_shape=[
            *[jax.ShapeDtypeStruct((PIECE, HALF), jnp.bfloat16)] * 4,
            jax.ShapeDtypeStruct((2, SEG, FEATURES), jnp.bfloat16),
            jax.ShapeDtypeStruct((2, SEG, FEATURES), jnp.bfloat16),
        ],
        compiler_params=PARAMS,
        cost_estimate=cost(0, 12 * 2**20),
        name="prepare",
    )(meta, weight, cot)


def tie_kernel(*refs):
    pass


def tie(*arrays):
    return pl.pallas_call(
        tie_kernel,
        in_specs=[ANY] * len(arrays),
        out_specs=[ANY] * len(arrays),
        out_shape=[jax.ShapeDtypeStruct(a.shape, a.dtype) for a in arrays],
        input_output_aliases={i: i for i in range(len(arrays))},
        name="tie",
    )(*arrays)


def blocks_kernel(count, added, meta, *refs):
    cots, weights, refs = refs[:count], refs[count : 2 * count], refs[2 * count :]
    total = sum(
        lax.dot_general(
            cot[...].reshape(2 * SEG, FEATURES), weight[...], NT, preferred_element_type=jnp.float32
        )
        for cot, weight in zip(cots, weights)
    ).reshape(2, SEG, ROWS)
    if added:
        total += refs[0][...]
    refs[-2][...] = total.astype(refs[-2].dtype)
    refs[-1][...] = jnp.zeros(TOKEN_SHAPE.shape, jnp.float32)


def feature_spec(step):
    def index(n, meta):
        return n, meta[3] * 4 + lax.rem(meta[4] + step, 4)

    return pl.BlockSpec((ROWS, FEATURES), index)


def blocks_product(meta, cots, steps, weight, earlier, dtype, token):
    count = len(cots)
    whole = pl.BlockSpec((2, SEG, FEATURES), lambda n, *_: (0, 0, 0))
    part = pl.BlockSpec((2, SEG, ROWS), lambda n, *_: (0, 0, n))
    return pl.pallas_call(
        functools.partial(blocks_kernel, count, len(earlier)),
        grid_spec=pltpu.PrefetchScalarGridSpec(
            num_scalar_prefetch=1,
            grid=(4,),
            in_specs=[whole] * count
            + [feature_spec(step) for step in steps]
            + [part] * len(earlier)
            + [ANY],
            out_specs=[part, TOKEN],
        ),
        out_shape=[jax.ShapeDtypeStruct((2, SEG, FEATURES), dtype), TOKEN_SHAPE],
        compiler_params=LARGE,
        cost_estimate=cost(count * SEG * 1024 * HALF, 2 * 1024 * HALF),
        name="own_product",
    )(meta, *cots, *[weight] * count, *earlier, token)


def product_kernel(meta, own, above, below, across, *refs):
    weights, refs = refs[:8], refs[8:]
    outs, token, (cots, held, cot_sems, sems) = refs[1:3], refs[3], refs[4:]
    step = pl.program_id(0)

    def place(source, offset, sem, rows):
        column = pl.multiple_of(lax.rem(meta[4] + offset, 4) * FEATURES, FEATURES)
        target = cots.at[rows, pl.ds(column, FEATURES)]
        return pltpu.make_async_copy(source, target, cot_sems.at[sem])

    def block(q):
        return [
            pltpu.make_async_copy(
                weights[2 * q + i], held.at[q, pl.ds(i * PIECE, PIECE)], sems.at[q, i]
            )
            for i in range(2)
        ]

    upper, lower = pl.ds(0, SEG), pl.ds(SEG, SEG)
    moves = [
        place(part.at[i], offset, 2 * k + i, rows)
        for k, (part, offset) in enumerate(((own, 0), (above, 1), (below, 3), (across, 2)))
        for i, rows in enumerate((upper, lower))
    ]
    blocks = [block(q) for q in range(4)]

    @pl.when(step == 0)
    def _():
        for move in moves + blocks[0]:
            move.start()
        for move in moves + blocks[0]:
            move.wait()
        for move in blocks[1] + blocks[2] + blocks[3]:
            move.start()

    for q in range(1, 4):

        @pl.when(step == q)
        def _(q=q):
            for move in blocks[q]:
                move.wait()

    token[...] = jnp.zeros(TOKEN_SHAPE.shape, jnp.float32)
    total = lax.dot_general(cots[...], held[step], NT, preferred_element_type=jnp.float32)
    for i in range(2):
        part = total[i * SEG : (i + 1) * SEG]
        outs[i][0] = part[:, :PIECE].astype(jnp.bfloat16)
        outs[i][1] = part[:, PIECE:].astype(jnp.bfloat16)


def product(meta, cots, weights, token):
    out_shape = [jax.ShapeDtypeStruct((8, SEG, PIECE), jnp.bfloat16)] * 2 + [TOKEN_SHAPE]
    out_specs = [pl.BlockSpec((2, SEG, PIECE), lambda q, *_: (q, 0, 0))] * 2 + [TOKEN]
    return pl.pallas_call(
        product_kernel,
        grid_spec=pltpu.PrefetchScalarGridSpec(
            num_scalar_prefetch=1,
            grid=(4,),
            in_specs=[FREE] * 4 + [ANY] * 4 + [FREE] * 4 + [ANY],
            out_specs=out_specs,
            scratch_shapes=[
                pltpu.VMEM((2 * SEG, HALF), jnp.bfloat16),
                pltpu.VMEM((4, ROWS, HALF), jnp.bfloat16),
                pltpu.SemaphoreType.DMA((8,)),
                pltpu.SemaphoreType.DMA((4, 2)),
            ],
        ),
        out_shape=out_shape,
        compiler_params=LIGHT,
        cost_estimate=cost(4 * SEG * 1024 * HALF, 2 * 1024 * HALF + 8 * SEG * 1024),
        name="partner_product",
    )(meta, *cots, *weights, token)


def pair_index(level, target):
    return level * (level - 1) // 2 + target


PAIRS = [(level, m) for level in range(LEVELS) for m in range(level)]


def pick_kernel(meta, parents, mine, *refs):
    outs, sems = refs[:2], refs[2]
    copies = []
    for i, (level, m) in enumerate(PAIRS):
        for side in range(2):
            me = node_id(meta)
            if side:
                me = me + 1 - 2 * meta[2]
            c, x, zh = relative(meta, ancestor(parents, me, level, m))
            for part in range(2):
                copy = pltpu.make_async_copy(
                    mine.at[x, zh, part, m], outs[side].at[i, part], sems.at[side, i, part]
                )
                copies.append((c == 0, copy))
    for held, copy in copies:
        pl.when(held)(copy.start)
    for held, copy in copies:
        pl.when(held)(copy.wait)


def pick(meta, parents, mine):
    shape = (len(PAIRS), 2, SEG, HD)
    return pl.pallas_call(
        pick_kernel,
        grid_spec=pltpu.PrefetchScalarGridSpec(
            num_scalar_prefetch=2,
            grid=(1,),
            in_specs=[ANY],
            out_specs=[pl.BlockSpec(shape, lambda *_: (0, 0, 0, 0))] * 2,
            scratch_shapes=[pltpu.SemaphoreType.DMA((2, len(PAIRS), 2))],
        ),
        out_shape=[jax.ShapeDtypeStruct(shape, jnp.bfloat16)] * 2,
        compiler_params=PARAMS,
        cost_estimate=cost(0, 0),
        name="pick",
    )(meta, parents, mine)


def probs_kernel(levels, meta, parents, lengths, query, own_key, own_value, *refs):
    count = len(levels)
    me = node_id(meta)
    if levels != (0,):
        (mine, other), refs = refs[:2], refs[2:]
        picked, sems = refs[-2:]
    refs = refs[1:]
    outs, averages, inverses = refs[:count], refs[count : 2 * count], refs[2 * count]

    @pl.when((pl.program_id(0) == 0) & (levels != (0,)))
    def _():
        copies = []
        for i, (level, m) in enumerate(PAIRS if levels != (0,) else []):
            c = relative(meta, ancestor(parents, me, level, m))[0]
            for part in range(2):
                pair = [
                    pltpu.make_async_copy(
                        source.at[i, part], picked.at[i, part], sems.at[i, part]
                    )
                    for source in (mine, other)
                ]
                pl.when(c == 0)(pair[0].start)
                pl.when(c == 1)(pair[1].start)
                copies.append(pair[0])
        for copy in copies:
            copy.wait()

    for k, level in enumerate(levels):
        q = jnp.concatenate(
            [query[level, 0, :, i * HD : (i + 1) * HD] for i in range(BATCH)], axis=0
        )
        blocks = []
        for m in range(level + 1):
            key = picked[pair_index(level, m), 0] if m < level else own_key[level, 0]
            s = lax.dot_general(key, q, NT, preferred_element_type=jnp.float32)
            length = lengths[m * NODES + ancestor(parents, me, level, m)]
            position = lax.broadcasted_iota(jnp.int32, s.shape, 0)
            allowed = position < length
            if m == level:
                asked = lax.broadcasted_iota(jnp.int32, s.shape, 1) & (SEG - 1)
                allowed = allowed & (position <= asked)
            blocks.append(jnp.where(allowed, s, MASKED))
        top = functools.reduce(
            jnp.maximum, [jnp.max(s, axis=0, keepdims=True) for s in blocks]
        )
        exps = [jnp.exp2((s - top) * EXP2_SCALE) for s in blocks]
        inverse = 1.0 / sum(jnp.sum(e, axis=0, keepdims=True) for e in exps)
        average = jnp.zeros((HD, BATCH * SEG), jnp.float32)
        for m in range(level + 1):
            narrow = exps[m].astype(jnp.bfloat16)
            outs[k][0, m * SEG : (m + 1) * SEG] = narrow
            value = picked[pair_index(level, m), 1] if m < level else own_value[level, 0]
            average += jnp.dot(
                value.astype(jnp.float32).T.astype(jnp.bfloat16),
                narrow,
                preferred_element_type=jnp.float32,
            )
        averages[k][...] = average * inverse
        inverses[level : level + 1] = inverse


def probs(levels, meta, parents, lengths, queries, key_rows, value_rows, gathered, token):
    width = BATCH * HD
    counts = [(level + 1) * SEG for level in levels]
    picked = (len(PAIRS), 2, SEG, HD)
    out_specs = [
        pl.BlockSpec((1, count, BATCH * SEG), lambda h, *_: (h, 0, 0)) for count in counts
    ]
    out_shape = [
        jax.ShapeDtypeStruct((GROUP // BATCH, count, BATCH * SEG), jnp.bfloat16)
        for count in counts
    ]
    out_specs += [pl.BlockSpec((HD, BATCH * SEG), lambda h, *_: (0, h))] * len(levels)
    out_shape += [jax.ShapeDtypeStruct((HD, GROUP * SEG), jnp.float32)] * len(levels)
    out_specs.append(pl.BlockSpec((8, BATCH * SEG), lambda h, *_: (0, h)))
    out_shape.append(jax.ShapeDtypeStruct((8, GROUP * SEG), jnp.float32))
    scratch = []
    if gathered:
        out_specs.append(pl.BlockSpec(picked, lambda h, *_: (0, 0, 0, 0)))
        out_shape.append(jax.ShapeDtypeStruct(picked, jnp.bfloat16))
        scratch.append(pltpu.SemaphoreType.DMA((len(PAIRS), 2)))
    own = pl.BlockSpec((LEVELS, 1, SEG, HD), lambda h, *_: (0, 0, 0, 0))
    return pl.pallas_call(
        functools.partial(probs_kernel, levels),
        grid_spec=pltpu.PrefetchScalarGridSpec(
            num_scalar_prefetch=3,
            grid=(GROUP // BATCH,),
            in_specs=[
                pl.BlockSpec((LEVELS, 1, SEG, width), lambda h, *_: (0, 0, 0, h)),
                own,
                own,
                *[ANY] * (len(gathered) + 1),
            ],
            out_specs=out_specs,
            scratch_shapes=scratch,
        ),
        out_shape=out_shape,
        compiler_params=PARAMS,
        cost_estimate=cost(0, 0),
        name="probs",
    )(meta, parents, lengths, queries, key_rows, value_rows, *gathered, token)


def backward_kernel(
    level, arrived, meta, parents, lengths, probs_ref, average, inverse, query, own, partner, own_key,
    own_value, *refs
):
    if level:
        picked, refs = refs[0], refs[1:]
    refs = refs[2 + arrived :]
    if level:
        query_out, own_out, ancestor_out, flipped, key_total, value_total = refs
    else:
        query_out, own_out, flipped, key_total, value_total = refs
    first = pair_index(level, 0)
    step = pl.program_id(0)
    blocks = [slice(m * SEG, (m + 1) * SEG) for m in range(level + 1)]

    @pl.when(step == 0)
    def _():
        key_total[...] = jnp.zeros_like(key_total)
        value_total[...] = jnp.zeros_like(value_total)
        for m in range(level + 1):
            key = picked[first + m, 0] if m < level else own_key[0, 0]
            flipped[:, blocks[m]] = key.astype(jnp.float32).T.astype(jnp.bfloat16)

    length = lengths[level * NODES + node_id(meta)]
    heads = []
    for i in range(BATCH):
        piece = lax.rem(step + meta[2], 2) * 4 + i
        total = own[0, :, i * HD : (i + 1) * HD].astype(jnp.float32)
        total += partner[piece].astype(jnp.float32)
        heads.append(total.astype(jnp.bfloat16).astype(jnp.float32).T)
    dout = jnp.concatenate(heads, axis=1)
    position = lax.broadcasted_iota(jnp.int32, dout.shape, 1) & (SEG - 1)
    dout = jnp.where(position < length, dout, 0.0) * inverse[level : level + 1]
    dout = dout.astype(jnp.bfloat16)
    delta = jnp.sum(dout.astype(jnp.float32) * average[...], axis=0, keepdims=True)
    q = jnp.concatenate([query[0, 0, :, i * HD : (i + 1) * HD] for i in range(BATCH)], axis=0)
    value = jnp.concatenate(
        [picked[first + m, 1] for m in range(level)] + [own_value[0, 0]], axis=0
    )
    narrow = probs_ref[0]
    grads = jnp.dot(value, dout, preferred_element_type=jnp.float32)
    scores = (narrow.astype(jnp.float32) * (grads - delta)).astype(jnp.bfloat16)
    key_total[...] += jnp.dot(scores, q, preferred_element_type=jnp.float32)
    value_total[...] += lax.dot_general(narrow, dout, NT, preferred_element_type=jnp.float32)
    query_total = jnp.dot(flipped[...], scores, preferred_element_type=jnp.float32) * SCALE
    for i in range(BATCH):
        part = query_total[:, i * SEG : (i + 1) * SEG]
        query_out[0, 0, :, i * HD : (i + 1) * HD] = part.T.astype(jnp.bfloat16)

    @pl.when(step == GROUP // BATCH - 1)
    def _():
        for m in range(level):
            ancestor_out[m, 0] = (key_total[blocks[m]] * SCALE).astype(jnp.bfloat16)
            ancestor_out[m, 1] = value_total[blocks[m]].astype(jnp.bfloat16)
        own_out[0] = key_total[blocks[level]] * SCALE
        own_out[1] = value_total[blocks[level]]


def backward(
    level, meta, parents, lengths, probabilities, average, inverse, queries, own, partner,
    key_rows, value_rows, picked, query_grad, token, arrived,
):
    count = (level + 1) * SEG
    width = BATCH * HD
    out_specs = [
        pl.BlockSpec((1, 1, SEG, width), lambda h, *_: (level, 0, 0, h)),
        pl.BlockSpec((2, SEG, HD), lambda h, *_: (0, 0, 0)),
    ]
    out_shape = [
        jax.ShapeDtypeStruct(queries.shape, jnp.bfloat16),
        jax.ShapeDtypeStruct((2, SEG, HD), jnp.float32),
    ]
    if level:
        out_specs.append(pl.BlockSpec((level, 2, SEG, HD), lambda h, *_: (0, 0, 0, 0)))
        out_shape.append(jax.ShapeDtypeStruct((level, 2, SEG, HD), jnp.bfloat16))
    last = level == LEVELS - 1
    return pl.pallas_call(
        functools.partial(backward_kernel, level, len(arrived)),
        grid_spec=pltpu.PrefetchScalarGridSpec(
            num_scalar_prefetch=3,
            grid=(GROUP // BATCH,),
            in_specs=[
                pl.BlockSpec((1, count, BATCH * SEG), lambda h, *_: (h, 0, 0)),
                pl.BlockSpec((HD, BATCH * SEG), lambda h, *_: (0, h)),
                pl.BlockSpec((8, BATCH * SEG), lambda h, *_: (0, h)),
                pl.BlockSpec((1, 1, SEG, width), lambda h, *_: (level, 0, 0, h)),
                pl.BlockSpec((1, SEG, width), lambda h, *_: (level % 2, 0, h)),
                pl.BlockSpec((8, SEG, PIECE), lambda h, *_: (0, 0, 0)),
                pl.BlockSpec((1, 1, SEG, HD), lambda h, *_: (level, 0, 0, 0)),
                pl.BlockSpec((1, 1, SEG, HD), lambda h, *_: (level, 0, 0, 0)),
            ]
            + [pl.BlockSpec((len(PAIRS), 2, SEG, HD), lambda h, *_: (0, 0, 0, 0))] * min(level, 1)
            + [ANY] * 2
            + [FREE] * len(arrived),
            out_specs=out_specs,
            scratch_shapes=[
                pltpu.VMEM((HD, count), jnp.bfloat16),
                pltpu.VMEM((count, HD), jnp.float32),
                pltpu.VMEM((count, HD), jnp.float32),
            ],
        ),
        out_shape=out_shape,
        input_output_aliases={} if last else {12 if level else 11: 0},
        compiler_params=MIDDLE,
        cost_estimate=cost(8 * GROUP * count * SEG * HD, 2 * GROUP * count * SEG),
        name=f"backward_{level}",
    )(
        meta, parents, lengths, probabilities, average, inverse, queries, own, partner,
        key_rows, value_rows, *[picked] * min(level, 1), query_grad, token,
        *arrived,
    )


def spread_kernel(targets, meta, parents, *refs):
    terms, outs, token = refs[:-6], refs[-5:-1], refs[-1]
    me = node_id(meta)
    sibling = me + 1 - 2 * meta[2]
    lowest = min(targets)
    token[...] = jnp.zeros(TOKEN_SHAPE.shape, jnp.float32)
    for j, target in enumerate(targets):
        found = []
        for i, term in enumerate(terms):
            level = lowest + 1 + i // 2
            if level > target:
                place = ancestor(parents, sibling if i % 2 else me, level, target)
                found.append((place, term[target].astype(jnp.float32)))
        for step, out in enumerate(outs):
            x = lax.rem(meta[1] + step, 4)
            for zh in range(2):
                wanted = (zh * 4 + x) * 2 + meta[2]
                total = sum(jnp.where(place == wanted, term, 0.0) for place, term in found)
                out[j, zh] = total.astype(jnp.bfloat16)


def spread(targets, meta, parents, terms, token):
    shape = (len(targets), 2, 2, SEG, HD)
    return pl.pallas_call(
        functools.partial(spread_kernel, targets),
        grid_spec=pltpu.PrefetchScalarGridSpec(
            num_scalar_prefetch=2,
            grid=(1,),
            in_specs=[pl.BlockSpec(term.shape, lambda *_: (0, 0, 0, 0)) for term in terms] + [FREE],
            out_specs=[pl.BlockSpec(shape, lambda *_: (0, 0, 0, 0, 0))] * 4 + [TOKEN],
        ),
        out_shape=[jax.ShapeDtypeStruct(shape, jnp.bfloat16)] * 4 + [TOKEN_SHAPE],
        compiler_params=SMALL,
        cost_estimate=cost(0, 0),
        name="spread",
    )(meta, parents, *terms, token)


def collect_kernel(meta, *refs):
    parts, (kept, given, token) = refs[:4], refs[5:]
    token[...] = jnp.zeros(TOKEN_SHAPE.shape, jnp.float32)
    for j in range(kept.shape[0]):
        kept[j] = sum(part[j, meta[0]].astype(jnp.float32) for part in parts)
        sent = sum(part[j, 1 - meta[0]].astype(jnp.float32) for part in parts)
        given[j] = sent.astype(jnp.bfloat16)


def collect(meta, parts, token):
    shape = parts[0].shape
    half = (shape[0], *shape[2:])
    return pl.pallas_call(
        collect_kernel,
        grid_spec=pltpu.PrefetchScalarGridSpec(
            num_scalar_prefetch=1,
            grid=(1,),
            in_specs=[pl.BlockSpec(shape, lambda *_: (0, 0, 0, 0, 0))] * 4 + [FREE],
            out_specs=[pl.BlockSpec(half, lambda *_: (0, 0, 0, 0))] * 2 + [TOKEN],
        ),
        out_shape=[
            jax.ShapeDtypeStruct(half, jnp.float32),
            jax.ShapeDtypeStruct(half, jnp.bfloat16),
            TOKEN_SHAPE,
        ],
        compiler_params=SMALL,
        cost_estimate=cost(0, 0),
        name="collect",
    )(meta, *parts, token)


def finish_kernel(*refs):
    owns, terms, outs = refs[:LEVELS], refs[LEVELS:8], refs[8:]
    for t in range(LEVELS):
        total = owns[t][...]
        if t < LEVELS - 1:
            for term in terms[2:] if t == 0 else terms[:2]:
                total += term[0 if t == 0 else 2 - t].astype(jnp.float32)
        for i in range(2):
            outs[i][t, 0] = total[i].astype(jnp.bfloat16)


def finish(owns, terms, shape):
    arrays = [*owns, *terms]
    return pl.pallas_call(
        finish_kernel,
        grid=(1,),
        in_specs=[
            pl.BlockSpec(array.shape, functools.partial(lambda rank, *_: (0,) * rank, array.ndim))
            for array in arrays
        ],
        out_specs=[pl.BlockSpec((LEVELS, 1, SEG, HD), lambda *_: (0, 0, 0, 0))] * 2,
        out_shape=[jax.ShapeDtypeStruct(shape, jnp.bfloat16)] * 2,
        compiler_params=SMALL,
        cost_estimate=cost(0, 0),
        name="finish",
    )(*arrays)


def local(queries, key_rows, value_rows, cotangent, out_weight, parents, seg_len):
    zh, x, c, zl, y = [lax.axis_index(name) for name in ("zh", "x", "c", "zl", "y")]
    meta = jnp.stack([zh, x, c, zl, y]).astype(jnp.int32)
    parents = parents.reshape(-1)
    lengths = seg_len.reshape(-1)
    table = (meta, parents, lengths)
    rows = jnp.stack([key_rows[: LEVELS - 1, 0], value_rows[: LEVELS - 1, 0]])
    away = lax.ppermute(rows, "zh", SWAP)
    *pieces, upper, lower = prepare(meta, out_weight, cotangent)
    rows, away, upper, *pieces = tie(rows, away, upper, *pieces)
    mine = lax.all_gather(jnp.stack([rows, away]), "x")

    def hop(piece, i):
        if i % 2:
            return lax.ppermute(piece, ("zh", "zl"), ALT)
        return lax.ppermute(piece, "zl", SWAP)

    above = lax.ppermute(upper, "y", DOWN)
    below = lax.ppermute(upper, "y", UP)
    w0, w1 = hop(pieces[0], 0), hop(pieces[1], 1)
    first_high, token = blocks_product(meta, [upper], (0,), out_weight, [], jnp.float32, meta)
    first_low, token = blocks_product(meta, [lower], (0,), out_weight, [], jnp.float32, token)
    root, root_average, root_inverse = probs(
        (0,), *table, queries, key_rows, value_rows, [], token
    )
    above, below, w0, w1, lower, p2, p3, first_high, first_low, root = tie(
        above, below, w0, w1, lower, pieces[2], pieces[3], first_high, first_low, root
    )
    across = lax.ppermute(below, "y", UP)
    above_low = lax.ppermute(lower, "y", DOWN)
    w2, w3 = hop(p2, 2), hop(p3, 3)
    early, token = blocks_product(
        meta, [above, below], (1, 3), out_weight, [first_high], jnp.float32, meta
    )
    mine, early = tie(mine, early)
    mine, other = pick(meta, parents, mine)
    other = lax.ppermute(other, "c", SWAP)
    results = probs(
        (3, 2, 1), *table, queries, key_rows, value_rows, [mine, other], token
    )
    probabilities = [root, *results[2::-1]]
    averages = [root_average, *results[5:2:-1]]
    inverse, picked = results[6:]
    inverses = [root_inverse, inverse, inverse, inverse]
    across, above_low, w0, w1, w2, w3, lower, early, picked = tie(
        across, above_low, w0, w1, w2, w3, lower, early, picked
    )
    below_low = lax.ppermute(lower, "y", UP)
    across_low = lax.ppermute(above_low, "y", DOWN)
    cots_low = (lower, above_low, below_low, across_low)
    weights = [w0, w1, w2, w3]
    weights += [lax.ppermute(piece, "c", SWAP) for piece in weights]
    partners = [None] * LEVELS

    def partner_pair(i, cots, token):
        parts = product(meta, cots, weights, token)
        for j in (1, 0):
            partners[2 * i + j] = lax.ppermute(parts[j], "zl", SWAP)
        return parts[2]

    own_high, token = blocks_product(
        meta, [across], (2,), out_weight, [early], jnp.bfloat16, meta
    )
    token = partner_pair(1, (upper, above, below, across), token)
    token = partner_pair(0, cots_low, token)
    own_grads = [None] * LEVELS
    terms = [None] * 6

    def back(level, own, query_grad, token):
        query_grad, own_grads[level], *rest = backward(
            level, *table, probabilities[level], averages[level], inverses[level], queries, own,
            partners[level], key_rows, value_rows, picked, query_grad, token,
            [],
        )
        if level:
            terms[2 * level - 2] = rest[0]
            terms[2 * level - 1] = lax.ppermute(rest[0], "c", SWAP)
        return query_grad

    query_grad = back(3, own_high, token, token)
    query_grad = back(2, own_high, query_grad, token)

    def send(targets, token):
        here, up, across, down, token = spread(
            targets, meta, parents, terms[2 * min(targets) :], token
        )
        moved = [
            here,
            lax.ppermute(up, "x", UP),
            lax.ppermute(down, "x", DOWN),
            lax.ppermute(across, "x", ACROSS),
        ]
        return moved, token

    high, token = send((2, 1), own_grads[2])
    own_low, token = blocks_product(
        meta, cots_low[1:], (1, 3, 2), out_weight, [first_low], jnp.bfloat16, token
    )
    query_grad = back(1, own_low, query_grad, token)
    low, token = send((0,), own_grads[1])
    query_grad = back(0, own_low, query_grad, token)
    high, high_given, token = collect(meta, high, own_grads[0])
    high_given = lax.ppermute(high_given, "zh", SWAP)
    low, low_given, token = collect(meta, low, token)
    low_given = lax.ppermute(low_given, "zh", SWAP)
    key_grad, value_grad = finish(own_grads, [high, high_given, low, low_given], key_rows.shape)
    return (query_grad, key_grad, value_grad)


def solution(mesh):
    fine = Mesh(mesh.devices.reshape(2, 4, 2, 2, 4), ("zh", "x", "c", "zl", "y"))
    rows = P(None, AXES, None, ("zl", "y"))
    in_specs = (rows, rows, rows, rows, P(("zl", "y"), None), P(), P())
    return jax.shard_map(
        local, mesh=fine, in_specs=in_specs, out_specs=(rows, rows, rows), check_vma=False
    )
```

```python
import functools

import jax
import jax.numpy as jnp
from jax import lax
from jax.experimental import pallas as pl
from jax.experimental.pallas import tpu as pltpu
from jax.sharding import Mesh, PartitionSpec as P

HD = 128
SEG = 256
GROUP = 8
BATCH = 4
LEVELS = 4
NODES = 16
FEATURES = 1024
HALF = 4096
PIECE = 128
ROWS = 256
SCALE = 1.0 / HD**0.5
EXP2_SCALE = SCALE * 1.4426950408889634
MASKED = -1e30
NT = (((1,), (1,)), ((), ()))
PARAMS = pltpu.CompilerParams(vmem_limit_bytes=56 * 2**20)
SMALL = pltpu.CompilerParams(vmem_limit_bytes=16 * 2**20)
LIGHT = pltpu.CompilerParams(vmem_limit_bytes=24 * 2**20)
LARGE = pltpu.CompilerParams(vmem_limit_bytes=48 * 2**20)
MIDDLE = pltpu.CompilerParams(vmem_limit_bytes=32 * 2**20)
ANY = pl.BlockSpec(memory_space=pltpu.HBM)
FREE = pl.BlockSpec(memory_space=pl.ANY)
AXES = ("zh", "x", "c")
ALT = [(0, 3), (1, 2), (2, 1), (3, 0)]
SWAP = [(0, 1), (1, 0)]
UP = [(i, (i + 1) % 4) for i in range(4)]
DOWN = [(i, (i + 3) % 4) for i in range(4)]
ACROSS = [(i, (i + 2) % 4) for i in range(4)]


TOKEN = pl.BlockSpec((8, HD), lambda *_: (0, 0))
TOKEN_SHAPE = jax.ShapeDtypeStruct((8, HD), jnp.float32)


def cost(flops, size, exps=0):
    return pl.CostEstimate(flops=1, bytes_accessed=1, transcendentals=0)


def node_id(meta):
    return (meta[0] * 4 + meta[1]) * 2 + meta[2]


def ancestor(parents, node, level, target):
    for m in reversed(range(target, level)):
        node = parents[m * NODES + node]
    return node


def relative(meta, node):
    zh = lax.rem(node // 8 + meta[0], 2)
    x = lax.rem(node // 2, 4)
    c = lax.rem(lax.rem(node, 2) + meta[2], 2)
    return c, x, zh


def prepare_kernel(meta, weight, cot, *refs):
    pieces, (upper, lower), refs = refs[:4], refs[4:6], refs[6:]
    held, passed, in_sems, out_sems = refs

    def piece(step):
        row = pl.multiple_of((meta[2] * 4 + step) * PIECE, PIECE)
        column = pl.multiple_of((1 - meta[3]) * HALF, HALF)
        return weight.at[pl.ds(row, PIECE), pl.ds(column, HALF)]

    moves = [
        (cot.at[2:4, 0], passed.at[0], upper),
        (cot.at[0:2, 0], passed.at[1], lower),
    ] + [(piece(i), held.at[i], pieces[i]) for i in range(4)]
    reads = [
        pltpu.make_async_copy(source, middle, in_sems.at[i])
        for i, (source, middle, _) in enumerate(moves)
    ]
    writes = [
        pltpu.make_async_copy(middle, target, out_sems.at[i])
        for i, (_, middle, target) in enumerate(moves)
    ]
    for read in reads:
        read.start()
    for read, write in zip(reads, writes):
        read.wait()
        write.start()
    for write in writes:
        write.wait()


def prepare(meta, weight, cot):
    return pl.pallas_call(
        prepare_kernel,
        grid_spec=pltpu.PrefetchScalarGridSpec(
            num_scalar_prefetch=1,
            grid=(),
            in_specs=[ANY] * 2,
            out_specs=[ANY] * 6,
            scratch_shapes=[
                pltpu.VMEM((4, PIECE, HALF), jnp.bfloat16),
                pltpu.VMEM((2, 2, SEG, FEATURES), jnp.bfloat16),
                pltpu.SemaphoreType.DMA((6,)),
                pltpu.SemaphoreType.DMA((6,)),
            ],
        ),
        out_shape=[
            *[jax.ShapeDtypeStruct((PIECE, HALF), jnp.bfloat16)] * 4,
            jax.ShapeDtypeStruct((2, SEG, FEATURES), jnp.bfloat16),
            jax.ShapeDtypeStruct((2, SEG, FEATURES), jnp.bfloat16),
        ],
        compiler_params=PARAMS,
        cost_estimate=cost(0, 12 * 2**20),
        name="prepare",
    )(meta, weight, cot)


def tie_kernel(*refs):
    pass


def tie(*arrays):
    return pl.pallas_call(
        tie_kernel,
        in_specs=[ANY] * len(arrays),
        out_specs=[ANY] * len(arrays),
        out_shape=[jax.ShapeDtypeStruct(a.shape, a.dtype) for a in arrays],
        input_output_aliases={i: i for i in range(len(arrays))},
        name="tie",
    )(*arrays)


def blocks_kernel(count, added, meta, *refs):
    cots, weights, refs = refs[:count], refs[count : 2 * count], refs[2 * count :]
    total = sum(
        lax.dot_general(
            cot[...].reshape(2 * SEG, FEATURES), weight[...], NT, preferred_element_type=jnp.float32
        )
        for cot, weight in zip(cots, weights)
    ).reshape(2, SEG, ROWS)
    if added:
        total += refs[0][...]
    refs[-2][...] = total.astype(refs[-2].dtype)
    refs[-1][...] = jnp.zeros(TOKEN_SHAPE.shape, jnp.float32)


def feature_spec(step):
    def index(n, meta):
        return n, meta[3] * 4 + lax.rem(meta[4] + step, 4)

    return pl.BlockSpec((ROWS, FEATURES), index)


def blocks_product(meta, cots, steps, weight, earlier, dtype, token):
    count = len(cots)
    whole = pl.BlockSpec((2, SEG, FEATURES), lambda n, *_: (0, 0, 0))
    part = pl.BlockSpec((2, SEG, ROWS), lambda n, *_: (0, 0, n))
    return pl.pallas_call(
        functools.partial(blocks_kernel, count, len(earlier)),
        grid_spec=pltpu.PrefetchScalarGridSpec(
            num_scalar_prefetch=1,
            grid=(4,),
            in_specs=[whole] * count
            + [feature_spec(step) for step in steps]
            + [part] * len(earlier)
            + [ANY],
            out_specs=[part, TOKEN],
        ),
        out_shape=[jax.ShapeDtypeStruct((2, SEG, FEATURES), dtype), TOKEN_SHAPE],
        compiler_params=PARAMS if dtype == jnp.float32 else LARGE,
        cost_estimate=cost(count * SEG * 1024 * HALF, 2 * 1024 * HALF),
        name="own_product",
    )(meta, *cots, *[weight] * count, *earlier, token)


def product_kernel(meta, own, above, below, across, *refs):
    weights, refs = refs[:8], refs[8:]
    outs, token, (cots, held, cot_sems, sems) = refs[1:3], refs[3], refs[4:]
    step = pl.program_id(0)

    def place(source, offset, sem, rows):
        column = pl.multiple_of(lax.rem(meta[4] + offset, 4) * FEATURES, FEATURES)
        target = cots.at[rows, pl.ds(column, FEATURES)]
        return pltpu.make_async_copy(source, target, cot_sems.at[sem])

    def block(q):
        return [
            pltpu.make_async_copy(
                weights[2 * q + i], held.at[q, pl.ds(i * PIECE, PIECE)], sems.at[q, i]
            )
            for i in range(2)
        ]

    upper, lower = pl.ds(0, SEG), pl.ds(SEG, SEG)
    moves = [
        place(part.at[i], offset, 2 * k + i, rows)
        for k, (part, offset) in enumerate(((own, 0), (above, 1), (below, 3), (across, 2)))
        for i, rows in enumerate((upper, lower))
    ]
    blocks = [block(q) for q in range(4)]

    @pl.when(step == 0)
    def _():
        for move in moves + blocks[0]:
            move.start()
        for move in moves + blocks[0]:
            move.wait()
        for move in blocks[1] + blocks[2] + blocks[3]:
            move.start()

    for q in range(1, 4):

        @pl.when(step == q)
        def _(q=q):
            for move in blocks[q]:
                move.wait()

    token[...] = jnp.zeros(TOKEN_SHAPE.shape, jnp.float32)
    total = lax.dot_general(cots[...], held[step], NT, preferred_element_type=jnp.float32)
    for i in range(2):
        part = total[i * SEG : (i + 1) * SEG]
        outs[i][0] = part[:, :PIECE].astype(jnp.bfloat16)
        outs[i][1] = part[:, PIECE:].astype(jnp.bfloat16)


def product(meta, cots, weights, token):
    out_shape = [jax.ShapeDtypeStruct((8, SEG, PIECE), jnp.bfloat16)] * 2 + [TOKEN_SHAPE]
    out_specs = [pl.BlockSpec((2, SEG, PIECE), lambda q, *_: (q, 0, 0))] * 2 + [TOKEN]
    return pl.pallas_call(
        product_kernel,
        grid_spec=pltpu.PrefetchScalarGridSpec(
            num_scalar_prefetch=1,
            grid=(4,),
            in_specs=[FREE] * 4 + [ANY] * 4 + [FREE] * 4 + [ANY],
            out_specs=out_specs,
            scratch_shapes=[
                pltpu.VMEM((2 * SEG, HALF), jnp.bfloat16),
                pltpu.VMEM((4, ROWS, HALF), jnp.bfloat16),
                pltpu.SemaphoreType.DMA((8,)),
                pltpu.SemaphoreType.DMA((4, 2)),
            ],
        ),
        out_shape=out_shape,
        compiler_params=LIGHT,
        cost_estimate=cost(4 * SEG * 1024 * HALF, 2 * 1024 * HALF + 8 * SEG * 1024),
        name="partner_product",
    )(meta, *cots, *weights, token)


def pair_index(level, target):
    return level * (level - 1) // 2 + target


PAIRS = [(level, m) for level in range(LEVELS) for m in range(level)]


def pick_kernel(meta, parents, mine, *refs):
    outs, sems = refs[:2], refs[2]
    copies = []
    for i, (level, m) in enumerate(PAIRS):
        for side in range(2):
            me = node_id(meta)
            if side:
                me = me + 1 - 2 * meta[2]
            c, x, zh = relative(meta, ancestor(parents, me, level, m))
            for part in range(2):
                copy = pltpu.make_async_copy(
                    mine.at[x, zh, part, m], outs[side].at[i, part], sems.at[side, i, part]
                )
                copies.append((c == 0, copy))
    for held, copy in copies:
        pl.when(held)(copy.start)
    for held, copy in copies:
        pl.when(held)(copy.wait)


def pick(meta, parents, mine):
    shape = (len(PAIRS), 2, SEG, HD)
    return pl.pallas_call(
        pick_kernel,
        grid_spec=pltpu.PrefetchScalarGridSpec(
            num_scalar_prefetch=2,
            grid=(1,),
            in_specs=[ANY],
            out_specs=[pl.BlockSpec(shape, lambda *_: (0, 0, 0, 0))] * 2,
            scratch_shapes=[pltpu.SemaphoreType.DMA((2, len(PAIRS), 2))],
        ),
        out_shape=[jax.ShapeDtypeStruct(shape, jnp.bfloat16)] * 2,
        compiler_params=PARAMS,
        cost_estimate=cost(0, 0),
        name="pick",
    )(meta, parents, mine)


def probs_kernel(levels, meta, parents, lengths, query, own_key, own_value, *refs):
    count = len(levels)
    me = node_id(meta)
    if levels != (0,):
        (mine, other), refs = refs[:2], refs[2:]
        picked, sems = refs[-2:]
    refs = refs[1:]
    outs, averages, inverses = refs[:count], refs[count : 2 * count], refs[2 * count]

    @pl.when((pl.program_id(0) == 0) & (levels != (0,)))
    def _():
        copies = []
        for i, (level, m) in enumerate(PAIRS if levels != (0,) else []):
            c = relative(meta, ancestor(parents, me, level, m))[0]
            for part in range(2):
                pair = [
                    pltpu.make_async_copy(
                        source.at[i, part], picked.at[i, part], sems.at[i, part]
                    )
                    for source in (mine, other)
                ]
                pl.when(c == 0)(pair[0].start)
                pl.when(c == 1)(pair[1].start)
                copies.append(pair[0])
        for copy in copies:
            copy.wait()

    for k, level in enumerate(levels):
        q = jnp.concatenate(
            [query[level, 0, :, i * HD : (i + 1) * HD] for i in range(BATCH)], axis=0
        )
        blocks = []
        for m in range(level + 1):
            key = picked[pair_index(level, m), 0] if m < level else own_key[level, 0]
            s = lax.dot_general(key, q, NT, preferred_element_type=jnp.float32)
            length = lengths[m * NODES + ancestor(parents, me, level, m)]
            position = lax.broadcasted_iota(jnp.int32, s.shape, 0)
            allowed = position < length
            if m == level:
                asked = lax.broadcasted_iota(jnp.int32, s.shape, 1) & (SEG - 1)
                allowed = allowed & (position <= asked)
            blocks.append(jnp.where(allowed, s, MASKED))
        top = functools.reduce(
            jnp.maximum, [jnp.max(s, axis=0, keepdims=True) for s in blocks]
        )
        exps = [jnp.exp2((s - top) * EXP2_SCALE) for s in blocks]
        inverse = 1.0 / sum(jnp.sum(e, axis=0, keepdims=True) for e in exps)
        average = jnp.zeros((HD, BATCH * SEG), jnp.float32)
        for m in range(level + 1):
            narrow = exps[m].astype(jnp.bfloat16)
            outs[k][0, m * SEG : (m + 1) * SEG] = narrow
            value = picked[pair_index(level, m), 1] if m < level else own_value[level, 0]
            average += jnp.dot(
                value.astype(jnp.float32).T.astype(jnp.bfloat16),
                narrow,
                preferred_element_type=jnp.float32,
            )
        averages[k][...] = average * inverse
        inverses[level : level + 1] = inverse


def probs(levels, meta, parents, lengths, queries, key_rows, value_rows, gathered, token):
    width = BATCH * HD
    counts = [(level + 1) * SEG for level in levels]
    picked = (len(PAIRS), 2, SEG, HD)
    out_specs = [
        pl.BlockSpec((1, count, BATCH * SEG), lambda h, *_: (h, 0, 0)) for count in counts
    ]
    out_shape = [
        jax.ShapeDtypeStruct((GROUP // BATCH, count, BATCH * SEG), jnp.bfloat16)
        for count in counts
    ]
    out_specs += [pl.BlockSpec((HD, BATCH * SEG), lambda h, *_: (0, h))] * len(levels)
    out_shape += [jax.ShapeDtypeStruct((HD, GROUP * SEG), jnp.float32)] * len(levels)
    out_specs.append(pl.BlockSpec((8, BATCH * SEG), lambda h, *_: (0, h)))
    out_shape.append(jax.ShapeDtypeStruct((8, GROUP * SEG), jnp.float32))
    scratch = []
    if gathered:
        out_specs.append(pl.BlockSpec(picked, lambda h, *_: (0, 0, 0, 0)))
        out_shape.append(jax.ShapeDtypeStruct(picked, jnp.bfloat16))
        scratch.append(pltpu.SemaphoreType.DMA((len(PAIRS), 2)))
    own = pl.BlockSpec((LEVELS, 1, SEG, HD), lambda h, *_: (0, 0, 0, 0))
    return pl.pallas_call(
        functools.partial(probs_kernel, levels),
        grid_spec=pltpu.PrefetchScalarGridSpec(
            num_scalar_prefetch=3,
            grid=(GROUP // BATCH,),
            in_specs=[
                pl.BlockSpec((LEVELS, 1, SEG, width), lambda h, *_: (0, 0, 0, h)),
                own,
                own,
                *[ANY] * (len(gathered) + 1),
            ],
            out_specs=out_specs,
            scratch_shapes=scratch,
        ),
        out_shape=out_shape,
        compiler_params=PARAMS,
        cost_estimate=cost(0, 0),
        name="probs",
    )(meta, parents, lengths, queries, key_rows, value_rows, *gathered, token)


def backward_kernel(
    level, arrived, meta, parents, lengths, probs_ref, average, inverse, query, own, partner, own_key,
    own_value, *refs
):
    if level:
        picked, refs = refs[0], refs[1:]
    refs = refs[2 + arrived :]
    if level:
        query_out, own_out, ancestor_out, flipped, key_total, value_total = refs
    else:
        query_out, own_out, flipped, key_total, value_total = refs
    first = pair_index(level, 0)
    step = pl.program_id(0)
    blocks = [slice(m * SEG, (m + 1) * SEG) for m in range(level + 1)]

    @pl.when(step == 0)
    def _():
        key_total[...] = jnp.zeros_like(key_total)
        value_total[...] = jnp.zeros_like(value_total)
        for m in range(level + 1):
            key = picked[first + m, 0] if m < level else own_key[0, 0]
            flipped[:, blocks[m]] = key.astype(jnp.float32).T.astype(jnp.bfloat16)

    length = lengths[level * NODES + node_id(meta)]
    heads = []
    for i in range(BATCH):
        piece = lax.rem(step + meta[2], 2) * 4 + i
        total = own[0, :, i * HD : (i + 1) * HD].astype(jnp.float32)
        total += partner[piece].astype(jnp.float32)
        heads.append(total.astype(jnp.bfloat16).astype(jnp.float32).T)
    dout = jnp.concatenate(heads, axis=1)
    position = lax.broadcasted_iota(jnp.int32, dout.shape, 1) & (SEG - 1)
    dout = jnp.where(position < length, dout, 0.0) * inverse[level : level + 1]
    dout = dout.astype(jnp.bfloat16)
    delta = jnp.sum(dout.astype(jnp.float32) * average[...], axis=0, keepdims=True)
    q = jnp.concatenate([query[0, 0, :, i * HD : (i + 1) * HD] for i in range(BATCH)], axis=0)
    value = jnp.concatenate(
        [picked[first + m, 1] for m in range(level)] + [own_value[0, 0]], axis=0
    )
    narrow = probs_ref[0]
    grads = jnp.dot(value, dout, preferred_element_type=jnp.float32)
    scores = (narrow.astype(jnp.float32) * (grads - delta)).astype(jnp.bfloat16)
    key_total[...] += jnp.dot(scores, q, preferred_element_type=jnp.float32)
    value_total[...] += lax.dot_general(narrow, dout, NT, preferred_element_type=jnp.float32)
    query_total = jnp.dot(flipped[...], scores, preferred_element_type=jnp.float32) * SCALE
    for i in range(BATCH):
        part = query_total[:, i * SEG : (i + 1) * SEG]
        query_out[0, 0, :, i * HD : (i + 1) * HD] = part.T.astype(jnp.bfloat16)

    @pl.when(step == GROUP // BATCH - 1)
    def _():
        for m in range(level):
            ancestor_out[m, 0] = (key_total[blocks[m]] * SCALE).astype(jnp.bfloat16)
            ancestor_out[m, 1] = value_total[blocks[m]].astype(jnp.bfloat16)
        own_out[0] = key_total[blocks[level]] * SCALE
        own_out[1] = value_total[blocks[level]]


def backward(
    level, meta, parents, lengths, probabilities, average, inverse, queries, own, partner,
    key_rows, value_rows, picked, query_grad, token, arrived,
):
    count = (level + 1) * SEG
    width = BATCH * HD
    out_specs = [
        pl.BlockSpec((1, 1, SEG, width), lambda h, *_: (level, 0, 0, h)),
        pl.BlockSpec((2, SEG, HD), lambda h, *_: (0, 0, 0)),
    ]
    out_shape = [
        jax.ShapeDtypeStruct(queries.shape, jnp.bfloat16),
        jax.ShapeDtypeStruct((2, SEG, HD), jnp.float32),
    ]
    if level:
        out_specs.append(pl.BlockSpec((level, 2, SEG, HD), lambda h, *_: (0, 0, 0, 0)))
        out_shape.append(jax.ShapeDtypeStruct((level, 2, SEG, HD), jnp.bfloat16))
    last = level == LEVELS - 1
    return pl.pallas_call(
        functools.partial(backward_kernel, level, len(arrived)),
        grid_spec=pltpu.PrefetchScalarGridSpec(
            num_scalar_prefetch=3,
            grid=(GROUP // BATCH,),
            in_specs=[
                pl.BlockSpec((1, count, BATCH * SEG), lambda h, *_: (h, 0, 0)),
                pl.BlockSpec((HD, BATCH * SEG), lambda h, *_: (0, h)),
                pl.BlockSpec((8, BATCH * SEG), lambda h, *_: (0, h)),
                pl.BlockSpec((1, 1, SEG, width), lambda h, *_: (level, 0, 0, h)),
                pl.BlockSpec((1, SEG, width), lambda h, *_: (level % 2, 0, h)),
                pl.BlockSpec((8, SEG, PIECE), lambda h, *_: (0, 0, 0)),
                pl.BlockSpec((1, 1, SEG, HD), lambda h, *_: (level, 0, 0, 0)),
                pl.BlockSpec((1, 1, SEG, HD), lambda h, *_: (level, 0, 0, 0)),
            ]
            + [pl.BlockSpec((len(PAIRS), 2, SEG, HD), lambda h, *_: (0, 0, 0, 0))] * min(level, 1)
            + [ANY] * 2
            + [FREE] * len(arrived),
            out_specs=out_specs,
            scratch_shapes=[
                pltpu.VMEM((HD, count), jnp.bfloat16),
                pltpu.VMEM((count, HD), jnp.float32),
                pltpu.VMEM((count, HD), jnp.float32),
            ],
        ),
        out_shape=out_shape,
        input_output_aliases={} if last else {12 if level else 11: 0},
        compiler_params=MIDDLE,
        cost_estimate=cost(8 * GROUP * count * SEG * HD, 2 * GROUP * count * SEG),
        name=f"backward_{level}",
    )(
        meta, parents, lengths, probabilities, average, inverse, queries, own, partner,
        key_rows, value_rows, *[picked] * min(level, 1), query_grad, token,
        *arrived,
    )


def spread_kernel(targets, meta, parents, *refs):
    terms, outs, token = refs[:-6], refs[-5:-1], refs[-1]
    me = node_id(meta)
    sibling = me + 1 - 2 * meta[2]
    lowest = min(targets)
    token[...] = jnp.zeros(TOKEN_SHAPE.shape, jnp.float32)
    for j, target in enumerate(targets):
        found = []
        for i, term in enumerate(terms):
            level = lowest + 1 + i // 2
            if level > target:
                place = ancestor(parents, sibling if i % 2 else me, level, target)
                found.append((place, term[target].astype(jnp.float32)))
        for step, out in enumerate(outs):
            x = lax.rem(meta[1] + step, 4)
            for zh in range(2):
                wanted = (zh * 4 + x) * 2 + meta[2]
                total = sum(jnp.where(place == wanted, term, 0.0) for place, term in found)
                out[j, zh] = total.astype(jnp.bfloat16)


def spread(targets, meta, parents, terms, token):
    shape = (len(targets), 2, 2, SEG, HD)
    return pl.pallas_call(
        functools.partial(spread_kernel, targets),
        grid_spec=pltpu.PrefetchScalarGridSpec(
            num_scalar_prefetch=2,
            grid=(1,),
            in_specs=[pl.BlockSpec(term.shape, lambda *_: (0, 0, 0, 0)) for term in terms] + [FREE],
            out_specs=[pl.BlockSpec(shape, lambda *_: (0, 0, 0, 0, 0))] * 4 + [TOKEN],
        ),
        out_shape=[jax.ShapeDtypeStruct(shape, jnp.bfloat16)] * 4 + [TOKEN_SHAPE],
        compiler_params=SMALL,
        cost_estimate=cost(0, 0),
        name="spread",
    )(meta, parents, *terms, token)


def collect_kernel(meta, *refs):
    parts, (kept, given, token) = refs[:4], refs[5:]
    token[...] = jnp.zeros(TOKEN_SHAPE.shape, jnp.float32)
    for j in range(kept.shape[0]):
        kept[j] = sum(part[j, meta[0]].astype(jnp.float32) for part in parts)
        sent = sum(part[j, 1 - meta[0]].astype(jnp.float32) for part in parts)
        given[j] = sent.astype(jnp.bfloat16)


def collect(meta, parts, token):
    shape = parts[0].shape
    half = (shape[0], *shape[2:])
    return pl.pallas_call(
        collect_kernel,
        grid_spec=pltpu.PrefetchScalarGridSpec(
            num_scalar_prefetch=1,
            grid=(1,),
            in_specs=[pl.BlockSpec(shape, lambda *_: (0, 0, 0, 0, 0))] * 4 + [FREE],
            out_specs=[pl.BlockSpec(half, lambda *_: (0, 0, 0, 0))] * 2 + [TOKEN],
        ),
        out_shape=[
            jax.ShapeDtypeStruct(half, jnp.float32),
            jax.ShapeDtypeStruct(half, jnp.bfloat16),
            TOKEN_SHAPE,
        ],
        compiler_params=SMALL,
        cost_estimate=cost(0, 0),
        name="collect",
    )(meta, *parts, token)


def finish_kernel(*refs):
    owns, terms, outs = refs[:LEVELS], refs[LEVELS:8], refs[8:]
    for t in range(LEVELS):
        total = owns[t][...]
        if t < LEVELS - 1:
            for term in terms[2:] if t == 0 else terms[:2]:
                total += term[0 if t == 0 else 2 - t].astype(jnp.float32)
        for i in range(2):
            outs[i][t, 0] = total[i].astype(jnp.bfloat16)


def finish(owns, terms, shape):
    arrays = [*owns, *terms]
    return pl.pallas_call(
        finish_kernel,
        grid=(1,),
        in_specs=[
            pl.BlockSpec(array.shape, functools.partial(lambda rank, *_: (0,) * rank, array.ndim))
            for array in arrays
        ],
        out_specs=[pl.BlockSpec((LEVELS, 1, SEG, HD), lambda *_: (0, 0, 0, 0))] * 2,
        out_shape=[jax.ShapeDtypeStruct(shape, jnp.bfloat16)] * 2,
        compiler_params=SMALL,
        cost_estimate=cost(0, 0),
        name="finish",
    )(*arrays)


def local(queries, key_rows, value_rows, cotangent, out_weight, parents, seg_len):
    zh, x, c, zl, y = [lax.axis_index(name) for name in ("zh", "x", "c", "zl", "y")]
    meta = jnp.stack([zh, x, c, zl, y]).astype(jnp.int32)
    parents = parents.reshape(-1)
    lengths = seg_len.reshape(-1)
    table = (meta, parents, lengths)
    rows = jnp.stack([key_rows[: LEVELS - 1, 0], value_rows[: LEVELS - 1, 0]])
    away = lax.ppermute(rows, "zh", SWAP)
    *pieces, upper, lower = prepare(meta, out_weight, cotangent)
    rows, away, upper, *pieces = tie(rows, away, upper, *pieces)
    mine = lax.all_gather(jnp.stack([rows, away]), "x")

    def hop(piece, i):
        if i % 2:
            return lax.ppermute(piece, ("zh", "zl"), ALT)
        return lax.ppermute(piece, "zl", SWAP)

    above = lax.ppermute(upper, "y", DOWN)
    below = lax.ppermute(upper, "y", UP)
    w0, w1 = hop(pieces[0], 0), hop(pieces[1], 1)
    first_high, token = blocks_product(meta, [upper], (0,), out_weight, [], jnp.float32, meta)
    first_low, token = blocks_product(meta, [lower], (0,), out_weight, [], jnp.float32, token)
    root, root_average, root_inverse = probs(
        (0,), *table, queries, key_rows, value_rows, [], token
    )
    above, below, w0, w1, lower, p2, p3, first_high, first_low, root = tie(
        above, below, w0, w1, lower, pieces[2], pieces[3], first_high, first_low, root
    )
    across = lax.ppermute(below, "y", UP)
    above_low = lax.ppermute(lower, "y", DOWN)
    w2, w3 = hop(p2, 2), hop(p3, 3)
    early, token = blocks_product(
        meta, [above, below], (1, 3), out_weight, [first_high], jnp.float32, meta
    )
    mine, early = tie(mine, early)
    mine, other = pick(meta, parents, mine)
    other = lax.ppermute(other, "c", SWAP)
    results = probs(
        (3, 2, 1), *table, queries, key_rows, value_rows, [mine, other], token
    )
    probabilities = [root, *results[2::-1]]
    averages = [root_average, *results[5:2:-1]]
    inverse, picked = results[6:]
    inverses = [root_inverse, inverse, inverse, inverse]
    across, above_low, w0, w1, w2, w3, lower, early, picked = tie(
        across, above_low, w0, w1, w2, w3, lower, early, picked
    )
    below_low = lax.ppermute(lower, "y", UP)
    across_low = lax.ppermute(above_low, "y", DOWN)
    cots_low = (lower, above_low, below_low, across_low)
    weights = [w0, w1, w2, w3]
    weights += [lax.ppermute(piece, "c", SWAP) for piece in weights]
    partners = [None] * LEVELS

    def partner_pair(i, cots, token):
        parts = product(meta, cots, weights, token)
        for j in (1, 0):
            partners[2 * i + j] = lax.ppermute(parts[j], "zl", SWAP)
        return parts[2]

    own_high, token = blocks_product(
        meta, [across], (2,), out_weight, [early], jnp.bfloat16, meta
    )
    token = partner_pair(1, (upper, above, below, across), token)
    token = partner_pair(0, cots_low, token)
    own_grads = [None] * LEVELS
    terms = [None] * 6

    def back(level, own, query_grad, token):
        query_grad, own_grads[level], *rest = backward(
            level, *table, probabilities[level], averages[level], inverses[level], queries, own,
            partners[level], key_rows, value_rows, picked, query_grad, token,
            [],
        )
        if level:
            terms[2 * level - 2] = rest[0]
            terms[2 * level - 1] = lax.ppermute(rest[0], "c", SWAP)
        return query_grad

    query_grad = back(3, own_high, token, token)
    query_grad = back(2, own_high, query_grad, token)

    def send(targets, token):
        here, up, across, down, token = spread(
            targets, meta, parents, terms[2 * min(targets) :], token
        )
        moved = [
            here,
            lax.ppermute(up, "x", UP),
            lax.ppermute(down, "x", DOWN),
            lax.ppermute(across, "x", ACROSS),
        ]
        return moved, token

    high, token = send((2, 1), own_grads[2])
    own_low, token = blocks_product(
        meta, cots_low[1:], (1, 3, 2), out_weight, [first_low], jnp.bfloat16, token
    )
    query_grad = back(1, own_low, query_grad, token)
    low, token = send((0,), own_grads[1])
    query_grad = back(0, own_low, query_grad, token)
    high, high_given, token = collect(meta, high, own_grads[0])
    high_given = lax.ppermute(high_given, "zh", SWAP)
    low, low_given, token = collect(meta, low, token)
    low_given = lax.ppermute(low_given, "zh", SWAP)
    key_grad, value_grad = finish(own_grads, [high, high_given, low, low_given], key_rows.shape)
    return (query_grad, key_grad, value_grad)


def solution(mesh):
    fine = Mesh(mesh.devices.reshape(2, 4, 2, 2, 4), ("zh", "x", "c", "zl", "y"))
    rows = P(None, AXES, None, ("zl", "y"))
    in_specs = (rows, rows, rows, rows, P(("zl", "y"), None), P(), P())
    return jax.shard_map(
        local, mesh=fine, in_specs=in_specs, out_specs=(rows, rows, rows), check_vma=False
    )
```
